32 devices in a mesh: row: 4 (over y, core), col: 4 (over z), win: 2 (over x).
Axes of the slice: x: 2, y: 2, z: 4, core: 2. Of those that a mesh axis runs over, the one named last changes fastest.
Arguments:
- spectra: bfloat16 [8, 32, 6144], P('win', 'row', 'col'), may hold values from -6 to 6
- usable: int32 [8, 32], replicated, may hold values 0 or 1
Outputs:
- stacked: float32 [32, 32, 9, 768], P(('row', 'win'), 'col')
The draws below stay inside these ranges and needn't reach their ends.
All inputs are finite; a program needn't handle non-finite values.
Results may differ from the reference program's by a relative error of at most 0.0046.
Values may be sent and summed in bfloat16 or wider, within the bound.
No kernel may reach another device: no remote copies, remote signals or barrier semaphores. Data moves between devices by JAX's collectives and lax.ppermute only.
A program may use at most 64 MiB of HBM per device.

```python
import math
import jax
import jax.numpy as jnp
from jax import lax

F = 1024
LAG = 768
DEC = 2
BLOCK = 8
WIN_DEV = 4
STATIONS = 32
WINDOWS = 8
N_ROW = 4
N_WIN = 2


def touch_ends(drawn, own_key, smallest, top_value):
    longest = drawn.shape.index(max(drawn.shape))
    spots = []
    for shift in (0, 1):
        where = [jax.random.randint(jax.random.fold_in(own_key, axis), (), 0, length) for axis, length in enumerate(drawn.shape)]
        where[longest] = (where[longest] + shift) % drawn.shape[longest]
        spots.append(tuple(where))
    return drawn.at[spots[0]].set(smallest).at[spots[1]].set(top_value)


def block_scale(own_key, dims, pieces, low, high):
    def one(position, parts):
        heights = jax.random.uniform(jax.random.fold_in(jax.random.fold_in(own_key, 6), position), (parts,), jnp.float32, low / len(pieces), high / len(pieces))
        return jnp.repeat(jnp.exp(heights), dims[position] // parts).reshape((-1,) + (1,) * (len(dims) - position - 1))

    gain = one(*pieces[0])
    for cut in pieces[1:]:
        gain = gain * one(*cut)
    return gain


def noise(own_key, dims, spread, reach, shards=(), held_as=jnp.bfloat16):
    entries = jax.random.normal(own_key, dims, jnp.float32) * spread
    if len(shards) > 0:
        entries = block_scale(own_key, dims, shards, -0.22, 0.18) * entries
    return jnp.clip(entries, min=-reach, max=reach).astype(held_as)


def setup_inputs(seed: int = 0) -> dict:
    streams_of = jax.random.split(jax.random.key(seed), 3)
    return {
        "spectra": noise(streams_of[0], (WINDOWS, STATIONS, 6 * F), 1.0, 6.0, ((0, 2), (1, 4), (2, 4))),
        "usable": touch_ends((jax.random.randint(streams_of[1], (WINDOWS, STATIONS), 0, 2) < 1).astype(jnp.int32), jax.random.fold_in(streams_of[1], 1), 0, 1),
    }


def build_table():
    frequency = jnp.arange(F, dtype=jnp.int32)
    lag_shift = DEC * (jnp.arange(LAG, dtype=jnp.int32) - LAG // 2)
    phase_index = frequency[:, None] * lag_shift[None, :] % (2 * F)
    phase_angle = phase_index.astype(jnp.float32) * (math.pi / F)
    scaling = 1.0 / math.sqrt(F)
    return jnp.concatenate([jnp.cos(phase_angle) * scaling, -jnp.sin(phase_angle) * scaling], 0).astype(jnp.bfloat16)

def lag_terms(row_part, col_part, dft_table):
    window_count, row_count = (row_part.shape[0], row_part.shape[1])
    col_count = col_part.shape[1]
    left_side = row_part.reshape(window_count, row_count, 3, 2, F).astype(jnp.float32)
    right_side = col_part.reshape(window_count, col_count, 3, 2, F).astype(jnp.float32)
    left_real = left_side[:, :, :, 0].reshape(window_count, row_count * 3, F)
    left_imag = left_side[:, :, :, 1].reshape(window_count, row_count * 3, F)
    right_real = right_side[:, :, :, 0].reshape(window_count, col_count * 3, F)
    right_imag = right_side[:, :, :, 1].reshape(window_count, col_count * 3, F)
    first_real = jnp.concatenate([left_real, left_imag], 0)
    second_real = jnp.concatenate([right_real, right_imag], 0)
    first_imag = jnp.concatenate([left_imag, left_real], 0)
    second_imag = jnp.concatenate([right_real, -right_imag], 0)
    real_part = jnp.einsum('wpf,wqf->pqf', first_real, second_real)
    imag_part = jnp.einsum('wpf,wqf->pqf', first_imag, second_imag)
    spectrum = jnp.stack([real_part, imag_part], 2).astype(jnp.bfloat16)
    flat_spectrum = spectrum.reshape(row_count * 3 * col_count * 3, 2 * F)
    lag_values = jnp.dot(flat_spectrum, dft_table, preferred_element_type=jnp.float32).astype(jnp.bfloat16)
    lag_values = lag_values.reshape(row_count, 3, col_count, 3, LAG).transpose(0, 2, 1, 3, 4)
    return lag_values.reshape(row_count, col_count, 9, LAG)

def reference(spectra, usable):
    dft_table = build_table()
    masked = spectra * usable[:, :, None].astype(jnp.bfloat16)
    window_parts = masked.reshape(N_WIN, WIN_DEV, STATIONS, 6 * F)
    weights = usable.astype(jnp.float32)
    pair_count = jnp.dot(weights.T, weights, precision=lax.Precision.HIGHEST)

    def one_block(row_start):
        stacked_sum = jnp.zeros((BLOCK, STATIONS, 9, LAG), jnp.float32)
        for half_index in range(N_WIN):
            row_part = lax.dynamic_slice_in_dim(window_parts[half_index], row_start, BLOCK, 1)
            stacked_sum = stacked_sum + lag_terms(row_part, window_parts[half_index], dft_table).astype(jnp.float32)
        block_count = lax.dynamic_slice_in_dim(pair_count, row_start, BLOCK, 0)
        return stacked_sum / jnp.maximum(block_count, 1.0)[:, :, None, None]
    block_starts = jnp.arange(N_ROW, dtype=jnp.int32) * BLOCK
    result = lax.map(one_block, block_starts)
    return result.reshape(STATIONS, STATIONS, 9, LAG)
```

```python
import math

import jax
import jax.numpy as jnp
import numpy as np
from jax import lax
from jax.experimental import pallas as pl
from jax.experimental.pallas import tpu as pltpu
from jax.sharding import PartitionSpec as P

F = 1024
LAG = 768
DEC = 2
LANES = 128
CHUNKS = F // LANES


def build_table():
    shift = DEC * (np.arange(LAG, dtype=np.int64) - LAG // 2)
    phase = (np.arange(F, dtype=np.int64)[:, None] * shift[None, :]) % (2 * F)
    angle = phase.astype(np.float64) * (math.pi / F)
    scale = 1.0 / math.sqrt(F)
    both = np.stack([np.cos(angle) * scale, -np.sin(angle) * scale])
    both = both.reshape(2, CHUNKS, LANES, LAG).transpose(1, 0, 2, 3)
    return both.reshape(2 * F, LAG).astype(np.float32).astype(jnp.bfloat16)


def make_kernel(windows, half, block):
    def kernel(rows_ref, cols_ref, rmask_ref, cmask_ref, inv_ref, table_ref, out_ref, left, right, cross):
        per_shard = rows_ref.shape[2] // LANES

        def place(part, chunk):
            piece = part * CHUNKS + chunk
            return piece // per_shard, (piece % per_shard) * LANES

        rmask = rmask_ref[...]
        cmask = cmask_ref[...]
        for part in range(6):
            for chunk in range(CHUNKS):
                shard, at = place(part, chunk)
                left[chunk, part] = rows_ref[shard, :, at : at + LANES].astype(jnp.float32) * rmask
                right[chunk, part] = cols_ref[shard, :, at : at + LANES].astype(jnp.float32) * cmask

        def one_chunk(chunk, carry):
            for b in range(3):
                col_re = [right[chunk, 2 * b, w * block : (w + 1) * block] for w in range(windows)]
                col_im = [right[chunk, 2 * b + 1, w * block : (w + 1) * block] for w in range(windows)]
                for a in range(3):
                    for pair in range(half // 2):
                        reals, imags = [], []
                        for s in (2 * pair, 2 * pair + 1):
                            re = im = None
                            for w in range(windows):
                                at = w * half + s
                                row_re = jnp.broadcast_to(left[chunk, 2 * a, at : at + 1], (block, LANES))
                                row_im = jnp.broadcast_to(left[chunk, 2 * a + 1, at : at + 1], (block, LANES))
                                new_re = row_re * col_re[w] + row_im * col_im[w]
                                new_im = row_im * col_re[w] - row_re * col_im[w]
                                re = new_re if re is None else re + new_re
                                im = new_im if im is None else im + new_im
                            reals.append(re)
                            imags.append(im)
                        first = ((pair * 3 + a) * 3 + b) * 2 * block
                        cross[chunk, first : first + 2 * block, :LANES] = jnp.concatenate(reals, 0).astype(jnp.bfloat16)
                        cross[chunk, first : first + 2 * block, LANES:] = jnp.concatenate(imags, 0).astype(jnp.bfloat16)
            return carry

        lax.fori_loop(0, CHUNKS, one_chunk, 0)
        total = None
        for chunk in range(CHUNKS):
            new = jnp.dot(
                cross[chunk], table_ref[2 * LANES * chunk : 2 * LANES * (chunk + 1)], preferred_element_type=jnp.float32
            )
            total = new if total is None else total + new
        for s in range(half):
            inv = inv_ref[s * block : (s + 1) * block, :1]
            for c in range(9):
                group = ((s // 2) * 9 + c) * 2 + s % 2
                out_ref[s, c] = total[group * block : (group + 1) * block] * inv

    return kernel


def correlate(rows, cols, rmask, cmask, inv, table, half, block):
    windows = rows.shape[1] // half
    groups = half * 9 * block
    return pl.pallas_call(
        make_kernel(windows, half, block),
        out_shape=jax.ShapeDtypeStruct((half, 9, block, LAG), jnp.float32),
        in_specs=[pl.BlockSpec(memory_space=pltpu.VMEM)] * 6,
        out_specs=pl.BlockSpec(memory_space=pltpu.VMEM),
        scratch_shapes=[
            pltpu.VMEM((CHUNKS, 6, windows * half, LANES), jnp.float32),
            pltpu.VMEM((CHUNKS, 6, windows * block, LANES), jnp.float32),
            pltpu.VMEM((CHUNKS, groups, 2 * LANES), jnp.bfloat16),
        ],
        compiler_params=pltpu.CompilerParams(vmem_limit_bytes=40 * 1024 * 1024),
        cost_estimate=pl.CostEstimate(flops=2 * groups * 2 * F * LAG, bytes_accessed=8 * 1024 * 1024, transcendentals=0),
    )(rows, cols, rmask, cmask, inv, table)


def body(spectra, usable):
    block = spectra.shape[1]
    shard = spectra.shape[2]
    n_row, n_col, n_win = (lax.axis_size(a) for a in ("row", "col", "win"))
    assert n_row == n_col
    half = block // n_win
    windows = n_win * spectra.shape[0]
    row_index, col_index, win_index = (lax.axis_index(a) for a in ("row", "col", "win"))

    every = lax.all_gather(spectra, "win", axis=0, tiled=True)
    pairs = [
        ((r * n_col + c) * n_win + w, (c * n_col + r) * n_win + w)
        for r in range(n_row)
        for c in range(n_col)
        for w in range(n_win)
    ]
    turned = lax.ppermute(every.reshape(windows * block, shard), ("row", "col", "win"), pairs)
    own = lax.dynamic_slice_in_dim(every, win_index * half, half, 1).reshape(windows * half, shard)
    rows = lax.all_gather(own, "col", axis=0)
    cols = lax.all_gather(turned, "row", axis=0)

    weights = usable.astype(jnp.float32)
    row_weights = lax.dynamic_slice_in_dim(weights, row_index * block + win_index * half, half, 1)
    col_weights = lax.dynamic_slice_in_dim(weights, col_index * block, block, 1)
    count = jnp.sum(row_weights[:, :, None] * col_weights[:, None, :], 0)
    inv = jnp.broadcast_to((1.0 / jnp.maximum(count, 1.0)).reshape(half * block, 1), (half * block, LANES))
    rmask = jnp.broadcast_to(row_weights.reshape(windows * half, 1), (windows * half, LANES))
    cmask = jnp.broadcast_to(col_weights.reshape(windows * block, 1), (windows * block, LANES))
    out = correlate(rows, cols, rmask, cmask, inv, jnp.asarray(build_table()), half, block)
    return out.transpose(0, 2, 1, 3)


def solution(mesh):
    placed = (P("win", "row", "col"), P())
    return jax.shard_map(
        body,
        mesh=mesh,
        in_specs=placed,
        out_specs=P(("row", "win"), "col", None, None),
        check_vma=False,
    )
```

```python
import math

import jax
import jax.numpy as jnp
import numpy as np
from jax import lax
from jax.experimental import pallas as pl
from jax.experimental.pallas import tpu as pltpu
from jax.sharding import PartitionSpec as P

F = 1024
LAG = 768
DEC = 2
LANES = 128
CHUNKS = F // LANES
AXES = ("row", "col", "win")


def build_table():
    shift = DEC * (np.arange(LAG, dtype=np.int64) - LAG // 2)
    phase = (np.arange(F, dtype=np.int64)[:, None] * shift[None, :]) % (2 * F)
    angle = phase.astype(np.float64) * (math.pi / F)
    scale = 1.0 / math.sqrt(F)
    both = np.stack([np.cos(angle) * scale, -np.sin(angle) * scale])
    both = both.reshape(2, CHUNKS, LANES, LAG).transpose(1, 0, 2, 3)
    return both.reshape(2 * F, LAG).astype(np.float32).astype(jnp.bfloat16)


def make_kernel(row_places, col_places, half, block, span):
    n_rows, n_cols = len(row_places), len(col_places)

    def kernel(*refs):
        row_slots, col_slots = refs[:n_rows], refs[n_rows : n_rows + n_cols]
        usable_hbm, table_hbm, out_ref, left, right, cross, rmask, cmask, usable_ref, flag_sem, table_ref, sem = refs[
            n_rows + n_cols :
        ]
        flags = pltpu.make_async_copy(usable_hbm, usable_ref, flag_sem)
        flags.start()
        fetch = pltpu.make_async_copy(table_hbm, table_ref, sem)
        fetch.start()
        at = tuple(lax.axis_index(a) for a in AXES)
        row, col, win = at
        per_shard = row_slots[0].shape[1] // LANES

        flags.wait()
        usable = usable_ref[...].astype(jnp.float32)
        stations = usable.shape[1]

        def column(first, count, h):
            rows = jnp.concatenate(
                [jnp.broadcast_to(usable[w : w + 1], (count, stations)) for w in range(h * span, (h + 1) * span)], 0
            )
            shape = (span * count, stations)
            picked = lax.broadcasted_iota(jnp.int32, shape, 1) == first + lax.broadcasted_iota(jnp.int32, shape, 0) % count
            return jnp.sum(jnp.where(picked, rows, 0.0), 1, keepdims=True)

        counts = [jnp.zeros((block, LANES), jnp.float32) for _ in range(half)]
        for h in range(2):
            rm = jnp.broadcast_to(column(row * block + win * half, half, h), (span * half, LANES))
            cm = jnp.broadcast_to(column(col * block, block, h), (span * block, LANES))
            rmask[h] = rm
            cmask[h] = cm
            for w in range(span):
                for s in range(half):
                    counts[s] = counts[s] + rm[w * half + s : w * half + s + 1] * cm[w * block : (w + 1) * block]
        invs = [1.0 / jnp.maximum(c, 1.0) for c in counts]

        for ref, place in zip(row_slots, row_places):
            shard = place(*at)
            for h in range(2):
                own = win if h == 0 else 1 - win
                mask = rmask[own]
                for i in range(per_shard):
                    data = ref[h * span * half : (h + 1) * span * half, i * LANES : (i + 1) * LANES]
                    left[shard * per_shard + i, own] = data.astype(jnp.float32) * mask
        for ref, place in zip(col_slots, col_places):
            shard, own = place(*at)
            mask = cmask[own]
            for i in range(per_shard):
                data = ref[:, i * LANES : (i + 1) * LANES]
                right[shard * per_shard + i, own] = data.astype(jnp.float32) * mask

        windows = [(h, w) for h in range(2) for w in range(span)]

        def one_chunk(chunk, carry):
            for b in range(3):
                col_re = [right[2 * b * CHUNKS + chunk, h, w * block : (w + 1) * block] for h, w in windows]
                col_im = [right[(2 * b + 1) * CHUNKS + chunk, h, w * block : (w + 1) * block] for h, w in windows]
                for a in range(3):
                    for pair in range(half // 2):
                        reals, imags = [], []
                        for s in (2 * pair, 2 * pair + 1):
                            re = im = None
                            for (h, w), c_re, c_im in zip(windows, col_re, col_im):
                                r = w * half + s
                                r_re = jnp.broadcast_to(left[2 * a * CHUNKS + chunk, h, r : r + 1], (block, LANES))
                                r_im = jnp.broadcast_to(left[(2 * a + 1) * CHUNKS + chunk, h, r : r + 1], (block, LANES))
                                new_re = r_re * c_re + r_im * c_im
                                new_im = r_im * c_re - r_re * c_im
                                re = new_re if re is None else re + new_re
                                im = new_im if im is None else im + new_im
                            reals.append(re)
                            imags.append(im)
                        first = ((pair * 3 + a) * 3 + b) * 2 * block
                        cross[chunk, first : first + 2 * block, :LANES] = jnp.concatenate(reals, 0).astype(jnp.bfloat16)
                        cross[chunk, first : first + 2 * block, LANES:] = jnp.concatenate(imags, 0).astype(jnp.bfloat16)
            return carry

        lax.fori_loop(0, CHUNKS, one_chunk, 0)
        fetch.wait()
        total = None
        for chunk in range(CHUNKS):
            new = jnp.dot(
                cross[chunk], table_ref[2 * LANES * chunk : 2 * LANES * (chunk + 1)], preferred_element_type=jnp.float32
            )
            total = new if total is None else total + new
        for s in range(half):
            for c in range(9):
                group = ((s // 2) * 9 + c) * 2 + s % 2
                out_ref[s, c] = total[group * block : (group + 1) * block] * invs[s][:, :1]

    return kernel


def correlate(rows, cols, usable, table, row_places, col_places, half, block, span):
    groups = half * 9 * block
    pieces = 6 * CHUNKS
    in_vmem = pl.BlockSpec(memory_space=pltpu.VMEM)
    return pl.pallas_call(
        make_kernel(row_places, col_places, half, block, span),
        out_shape=jax.ShapeDtypeStruct((half, 9, block, LAG), jnp.float32),
        in_specs=[in_vmem] * (len(rows) + len(cols)) + [pl.BlockSpec(memory_space=pltpu.HBM)] * 2,
        out_specs=in_vmem,
        scratch_shapes=[
            pltpu.VMEM((pieces, 2, span * half, LANES), jnp.float32),
            pltpu.VMEM((pieces, 2, span * block, LANES), jnp.float32),
            pltpu.VMEM((CHUNKS, groups, 2 * LANES), jnp.bfloat16),
            pltpu.VMEM((2, span * half, LANES), jnp.float32),
            pltpu.VMEM((2, span * block, LANES), jnp.float32),
            pltpu.VMEM(usable.shape, jnp.int32),
            pltpu.SemaphoreType.DMA,
            pltpu.VMEM(table.shape, jnp.bfloat16),
            pltpu.SemaphoreType.DMA,
        ],
        compiler_params=pltpu.CompilerParams(vmem_limit_bytes=40 * 1024 * 1024),
    )(*rows, *cols, usable, table)


def split_stations(spectra, half):
    span, block, shard = spectra.shape

    def kernel(spectra_ref, theirs_ref, mine_ref):
        low = [spectra_ref[w, :half] for w in range(span)]
        high = [spectra_ref[w, half:] for w in range(span)]
        first = lax.axis_index("win") == 0
        low, high = jnp.concatenate(low, 0), jnp.concatenate(high, 0)
        theirs_ref[...] = jnp.where(first, high, low)
        mine_ref[: span * half] = jnp.where(first, low, high)
        mine_ref[span * half :] = jnp.zeros((span * half, shard), jnp.bfloat16)

    in_vmem = pl.BlockSpec(memory_space=pltpu.VMEM)
    return pl.pallas_call(
        kernel,
        out_shape=(
            jax.ShapeDtypeStruct((span * half, shard), jnp.bfloat16),
            jax.ShapeDtypeStruct((2 * span * half, shard), jnp.bfloat16),
        ),
        in_specs=[in_vmem],
        out_specs=(in_vmem, in_vmem),
    )(spectra)


def body(spectra, usable):
    span, block, shard = spectra.shape
    n_row, n_col, n_win = (lax.axis_size(a) for a in AXES)
    assert n_row == n_col and n_win == 2
    half = block // n_win

    def send(data, move):
        pairs = []
        for r in range(n_row):
            for c in range(n_col):
                for w in range(n_win):
                    r2, c2, w2 = move(r, c, w)
                    pairs.append(((r * n_col + c) * n_win + w, (r2 * n_col + c2) * n_win + w2))
        return lax.ppermute(data, AXES, pairs)

    def other_win(r, c, w):
        return r, c, 1 - w

    flat = spectra.reshape(span * block, shard)
    turned = send(flat, lambda r, c, w: (n_row - 1 - c, r, w))
    theirs, mine = split_stations(spectra, half)
    got = send(theirs, other_win)
    mine = lax.dynamic_update_slice(mine, got, (span * half, 0))

    if n_row == 4:
        shifted = [send(mine, lambda r, c, w, k=k: (r, (c + k) % n_col, w)) for k in (2, 1, 3)]
        rows = [mine] + shifted
        row_places = [lambda r, c, w, k=k: lax.rem(c + n_col - k, n_col) for k in (0, 2, 1, 3)]
        near = [
            turned,
            send(turned, lambda r, c, w: (r ^ 2, c, w)),
            send(turned, other_win),
            send(turned, lambda r, c, w: (r ^ 2, c, 1 - w)),
        ]
        last = lax.optimization_barrier((near[3], *shifted))[0]
        cols = near + [send(x, lambda r, c, w: (r ^ 1, c, w)) for x in near[:3] + [last]]
        col_places = [
            lambda r, c, w, e=e, d=d: (n_row - 1 - (r ^ e), w ^ d)
            for e, d in ((0, 0), (2, 0), (0, 1), (2, 1), (1, 0), (3, 0), (1, 1), (3, 1))
        ]
    else:
        gathered = lax.all_gather(mine, "col", axis=0)
        rows = [gathered[i] for i in range(n_col)]
        row_places = [lambda r, c, w, i=i: i for i in range(n_col)]
        near = lax.all_gather(turned, "row", axis=0)
        far = send(near, other_win)
        cols = [x[i] for x in (near, far) for i in range(n_row)]
        col_places = [lambda r, c, w, i=i, d=d: (n_row - 1 - i, w ^ d) for d in range(2) for i in range(n_row)]

    out = correlate(rows, cols, usable, jnp.asarray(build_table()), row_places, col_places, half, block, span)
    return out.transpose(0, 2, 1, 3)


def solution(mesh):
    placed = (P("win", "row", "col"), P())
    return jax.shard_map(
        body,
        mesh=mesh,
        in_specs=placed,
        out_specs=P(("row", "win"), "col", None, None),
        check_vma=False,
    )
```

```python
import math

import jax
import jax.numpy as jnp
import numpy as np
from jax import lax
from jax.experimental import pallas as pl
from jax.experimental.pallas import tpu as pltpu
from jax.sharding import PartitionSpec as P

F = 1024
LAG = 768
DEC = 2
LANES = 128
CHUNKS = F // LANES
TILE = 256
AXES = ("row", "col", "win")


def build_table():
    shift = DEC * (np.arange(LAG, dtype=np.int64) - LAG // 2)
    phase = (np.arange(F, dtype=np.int64)[:, None] * shift[None, :]) % (2 * F)
    angle = phase.astype(np.float64) * (math.pi / F)
    scale = 1.0 / math.sqrt(F)
    both = np.stack([np.cos(angle) * scale, -np.sin(angle) * scale])
    both = both.reshape(2, CHUNKS, LANES, LAG).transpose(1, 0, 2, 3)
    return both.reshape(2 * F, LAG).astype(np.float32).astype(jnp.bfloat16)


def make_kernel(row_places, col_places, half, block, span):
    n_rows, n_cols = len(row_places), len(col_places)

    def kernel(*refs):
        row_slots, col_slots = refs[:n_rows], refs[n_rows : n_rows + n_cols]
        rmask, cmask, inv_ref, table_hbm, out_hbm, *scratch = refs[n_rows + n_cols :]
        left, right, cross, col_sum, col_diff, row_sum, staged, out_sem, table_ref, sem = scratch
        fetch = pltpu.make_async_copy(table_hbm, table_ref, sem)
        fetch.start()
        at = tuple(lax.axis_index(a) for a in AXES)
        win = at[2]
        per_shard = row_slots[0].shape[1] // LANES

        for ref, place in zip(row_slots, row_places):
            shard = place(*at)
            for h in range(2):
                own = win if h == 0 else 1 - win
                mask = rmask[own]
                for i in range(per_shard):
                    data = ref[h * span * half : (h + 1) * span * half, i * LANES : (i + 1) * LANES]
                    left[shard * per_shard + i, own] = data.astype(jnp.float32) * mask
        for ref, place in zip(col_slots, col_places):
            shard, own = place(*at)
            mask = cmask[own]
            for i in range(per_shard):
                data = ref[:, i * LANES : (i + 1) * LANES]
                right[shard * per_shard + i, own] = data.astype(jnp.float32) * mask

        windows = [(h, w) for h in range(2) for w in range(span)]

        def products(chunk, into):
            for b in range(3):
                for n, (h, w) in enumerate(windows):
                    c = right[2 * b * CHUNKS + chunk, h, w * block : (w + 1) * block]
                    e = right[(2 * b + 1) * CHUNKS + chunk, h, w * block : (w + 1) * block]
                    col_sum[b, n] = c + e
                    col_diff[b, n] = c - e
            for a in range(3):
                for h in range(2):
                    row_sum[a, h] = left[2 * a * CHUNKS + chunk, h] + left[(2 * a + 1) * CHUNKS + chunk, h]
            for a in range(3):
                one, two, three = {}, {}, {}
                for n, (h, w) in enumerate(windows):
                    c = [right[2 * b * CHUNKS + chunk, h, w * block : (w + 1) * block] for b in range(3)]
                    plus = [col_sum[b, n] for b in range(3)]
                    minus = [col_diff[b, n] for b in range(3)]
                    for s in range(half):
                        r = w * half + s
                        p = jnp.broadcast_to(left[2 * a * CHUNKS + chunk, h, r : r + 1], (block, LANES))
                        q = jnp.broadcast_to(left[(2 * a + 1) * CHUNKS + chunk, h, r : r + 1], (block, LANES))
                        pq = jnp.broadcast_to(row_sum[a, h, r : r + 1], (block, LANES))
                        for b in range(3):
                            x, y, z = pq * c[b], p * plus[b], q * minus[b]
                            one[s, b] = x if n == 0 else one[s, b] + x
                            two[s, b] = y if n == 0 else two[s, b] + y
                            three[s, b] = z if n == 0 else three[s, b] + z
                for pair in range(half // 2):
                    for b in range(3):
                        keys = [(2 * pair, b), (2 * pair + 1, b)]
                        re = jnp.concatenate([one[k] - three[k] for k in keys], 0).astype(jnp.bfloat16)
                        im = jnp.concatenate([one[k] - two[k] for k in keys], 0).astype(jnp.bfloat16)
                        first = ((pair * 3 + a) * 3 + b) * 2 * block
                        cross[into, first : first + 2 * block, :LANES] = re
                        cross[into, first : first + 2 * block, LANES:] = im

        def one_chunk(chunk, carry):
            products(chunk, chunk)
            return carry

        lax.fori_loop(0, CHUNKS, one_chunk, 0)
        fetch.wait()
        copies = []
        for n in range(LAG // TILE):
            acc = None
            for chunk in range(CHUNKS):
                new = jnp.dot(
                    cross[chunk],
                    table_ref[2 * LANES * chunk : 2 * LANES * (chunk + 1), n * TILE : (n + 1) * TILE],
                    preferred_element_type=jnp.float32,
                )
                acc = new if acc is None else acc + new
            for s in range(half):
                inv = inv_ref[s][:, :1]
                for c in range(9):
                    group = ((s // 2) * 9 + c) * 2 + s % 2
                    staged[n, s, c] = acc[group * block : (group + 1) * block] * inv
            copies.append(pltpu.make_async_copy(staged.at[n], out_hbm.at[:, :, :, pl.ds(n * TILE, TILE)], out_sem.at[n]))
            copies[-1].start()
        for copy in copies:
            copy.wait()

    return kernel


def masks(usable, half, block, span):
    def kernel(usable_ref, rmask, cmask, inv_ref):
        row, col, win = (lax.axis_index(a) for a in AXES)
        usable = usable_ref[...].astype(jnp.float32)
        stations = usable.shape[1]

        def column(first, count, h):
            rows = jnp.concatenate(
                [jnp.broadcast_to(usable[w : w + 1], (count, stations)) for w in range(h * span, (h + 1) * span)], 0
            )
            shape = (span * count, stations)
            picked = lax.broadcasted_iota(jnp.int32, shape, 1) == first + lax.broadcasted_iota(jnp.int32, shape, 0) % count
            return jnp.sum(jnp.where(picked, rows, 0.0), 1, keepdims=True)

        counts = [jnp.zeros((block, LANES), jnp.float32) for _ in range(half)]
        for h in range(2):
            rm = jnp.broadcast_to(column(row * block + win * half, half, h), (span * half, LANES))
            cm = jnp.broadcast_to(column(col * block, block, h), (span * block, LANES))
            rmask[h] = rm
            cmask[h] = cm
            for w in range(span):
                for s in range(half):
                    counts[s] = counts[s] + rm[w * half + s : w * half + s + 1] * cm[w * block : (w + 1) * block]
        for s in range(half):
            inv_ref[s] = 1.0 / jnp.maximum(counts[s], 1.0)

    in_vmem = pl.BlockSpec(memory_space=pltpu.VMEM)
    shapes = ((2, span * half, LANES), (2, span * block, LANES), (half, block, LANES))
    return pl.pallas_call(
        kernel,
        out_shape=tuple(jax.ShapeDtypeStruct(shape, jnp.float32) for shape in shapes),
        in_specs=[in_vmem],
        out_specs=(in_vmem,) * 3,
        compiler_params=pltpu.CompilerParams(vmem_limit_bytes=4 * 1024 * 1024),
    )(usable)


def correlate(rows, cols, flags, table, row_places, col_places, half, block, span):
    groups = half * 9 * block
    pieces = 6 * CHUNKS
    slots = len(rows) + len(cols) + 3
    hbm = pl.BlockSpec(memory_space=pltpu.HBM)
    return pl.pallas_call(
        make_kernel(row_places, col_places, half, block, span),
        out_shape=jax.ShapeDtypeStruct((half, 9, block, LAG), jnp.float32),
        in_specs=[pl.BlockSpec(memory_space=pltpu.VMEM)] * slots + [hbm],
        out_specs=hbm,
        scratch_shapes=[
            pltpu.VMEM((pieces, 2, span * half, LANES), jnp.float32),
            pltpu.VMEM((pieces, 2, span * block, LANES), jnp.float32),
            pltpu.VMEM((CHUNKS, groups, 2 * LANES), jnp.bfloat16),
            pltpu.VMEM((3, 2 * span, block, LANES), jnp.float32),
            pltpu.VMEM((3, 2 * span, block, LANES), jnp.float32),
            pltpu.VMEM((3, 2, span * half, LANES), jnp.float32),
            pltpu.VMEM((LAG // TILE, half, 9, block, TILE), jnp.float32),
            pltpu.SemaphoreType.DMA((LAG // TILE,)),
            pltpu.VMEM(table.shape, jnp.bfloat16),
            pltpu.SemaphoreType.DMA,
        ],
        compiler_params=pltpu.CompilerParams(vmem_limit_bytes=52 * 1024 * 1024),
    )(*rows, *cols, *flags, table)


def split_stations(spectra, half):
    span, block, shard = spectra.shape

    def kernel(spectra_ref, theirs_ref, mine_ref):
        low = [spectra_ref[w, :half] for w in range(span)]
        high = [spectra_ref[w, half:] for w in range(span)]
        first = lax.axis_index("win") == 0
        low, high = jnp.concatenate(low, 0), jnp.concatenate(high, 0)
        theirs_ref[...] = jnp.where(first, high, low)
        mine_ref[: span * half] = jnp.where(first, low, high)
        mine_ref[span * half :] = jnp.zeros((span * half, shard), jnp.bfloat16)

    in_vmem = pl.BlockSpec(memory_space=pltpu.VMEM)
    return pl.pallas_call(
        kernel,
        out_shape=(
            jax.ShapeDtypeStruct((span * half, shard), jnp.bfloat16),
            jax.ShapeDtypeStruct((2 * span * half, shard), jnp.bfloat16),
        ),
        in_specs=[in_vmem],
        out_specs=(in_vmem, in_vmem),
        compiler_params=pltpu.CompilerParams(vmem_limit_bytes=4 * 1024 * 1024),
    )(spectra)


def body(spectra, usable):
    span, block, shard = spectra.shape
    n_row, n_col, n_win = (lax.axis_size(a) for a in AXES)
    assert n_row == n_col and n_win == 2
    half = block // n_win

    def send(data, move):
        pairs = []
        for r in range(n_row):
            for c in range(n_col):
                for w in range(n_win):
                    r2, c2, w2 = move(r, c, w)
                    pairs.append(((r * n_col + c) * n_win + w, (r2 * n_col + c2) * n_win + w2))
        return lax.ppermute(data, AXES, pairs)

    def other_win(r, c, w):
        return r, c, 1 - w

    flat = spectra.reshape(span * block, shard)
    turned = send(flat, lambda r, c, w: (n_row - 1 - c, r, w))
    theirs, mine = split_stations(spectra, half)
    got = send(theirs, other_win)
    flags = masks(usable, half, block, span)
    mine, *flags = lax.optimization_barrier((mine, *flags))
    mine = lax.dynamic_update_slice(mine, got, (span * half, 0))

    if n_row == 4:
        across = send(mine, lambda r, c, w: (r, c ^ 2, w))
        beside = send(mine, lambda r, c, w: (r, c ^ 1, w))
        shifted = [across, beside, send(across, lambda r, c, w: (r, c ^ 1, w))]
        rows = [mine] + shifted
        row_places = [lambda r, c, w, k=k: c ^ k for k in (0, 2, 1, 3)]
        near = [
            turned,
            send(turned, lambda r, c, w: (r ^ 2, c, w)),
            send(turned, other_win),
            send(turned, lambda r, c, w: (r ^ 2, c, 1 - w)),
        ]
        last = lax.optimization_barrier((near[3], *shifted))[0]
        cols = near + [send(x, lambda r, c, w: (r ^ 1, c, w)) for x in near[:3] + [last]]
        col_places = [
            lambda r, c, w, e=e, d=d: (n_row - 1 - (r ^ e), w ^ d)
            for e, d in ((0, 0), (2, 0), (0, 1), (2, 1), (1, 0), (3, 0), (1, 1), (3, 1))
        ]
    else:
        gathered = lax.all_gather(mine, "col", axis=0)
        rows = [gathered[i] for i in range(n_col)]
        row_places = [lambda r, c, w, i=i: i for i in range(n_col)]
        near = lax.all_gather(turned, "row", axis=0)
        far = send(near, other_win)
        cols = [x[i] for x in (near, far) for i in range(n_row)]
        col_places = [lambda r, c, w, i=i, d=d: (n_row - 1 - i, w ^ d) for d in range(2) for i in range(n_row)]

    out = correlate(rows, cols, flags, jnp.asarray(build_table()), row_places, col_places, half, block, span)
    return out.transpose(0, 2, 1, 3)


def solution(mesh):
    placed = (P("win", "row", "col"), P())
    return jax.shard_map(
        body,
        mesh=mesh,
        in_specs=placed,
        out_specs=P(("row", "win"), "col", None, None),
        check_vma=False,
    )
```

```python
import math

import jax
import jax.numpy as jnp
import numpy as np
from jax import lax
from jax.experimental import pallas as pl
from jax.experimental.pallas import tpu as pltpu
from jax.sharding import PartitionSpec as P

F = 1024
LAG = 768
DEC = 2
LANES = 128
CHUNKS = F // LANES
TILE = 256
AXES = ("row", "col", "win")


def build_table():
    shift = DEC * (np.arange(LAG, dtype=np.int64) - LAG // 2)
    phase = (np.arange(F, dtype=np.int64)[:, None] * shift[None, :]) % (2 * F)
    angle = phase.astype(np.float64) * (math.pi / F)
    scale = 1.0 / math.sqrt(F)
    both = np.stack([np.cos(angle) * scale, -np.sin(angle) * scale])
    both = both.reshape(2, CHUNKS, LANES, LAG).transpose(1, 0, 2, 3)
    return both.reshape(2 * F, LAG).astype(np.float32).astype(jnp.bfloat16)


def make_kernel(row_places, col_places, half, block, span):
    n_rows, n_cols = len(row_places), len(col_places)

    def kernel(*refs):
        row_slots, col_slots = refs[:n_rows], refs[n_rows : n_rows + n_cols]
        rmask, cmask, inv_ref, table_hbm, out_hbm, *scratch = refs[n_rows + n_cols :]
        left, right, cross, col_sum, col_diff, row_sum, staged, out_sem, table_ref, sem = scratch
        fetch = pltpu.make_async_copy(table_hbm, table_ref, sem)
        fetch.start()
        at = tuple(lax.axis_index(a) for a in AXES)
        win = at[2]
        per_shard = row_slots[0].shape[1] // LANES

        for ref, place in zip(row_slots, row_places):
            shard = place(*at)
            for h in range(2):
                own = win if h == 0 else 1 - win
                mask = rmask[own]
                for i in range(per_shard):
                    data = ref[h * span * half : (h + 1) * span * half, i * LANES : (i + 1) * LANES]
                    left[shard * per_shard + i, own] = data.astype(jnp.float32) * mask
        for ref, place in zip(col_slots, col_places):
            shard, own = place(*at)
            mask = cmask[own]
            for i in range(per_shard):
                data = ref[:, i * LANES : (i + 1) * LANES]
                right[shard * per_shard + i, own] = data.astype(jnp.float32) * mask

        windows = [(h, w) for h in range(2) for w in range(span)]

        def products(chunk, into):
            for b in range(3):
                for n, (h, w) in enumerate(windows):
                    c = right[2 * b * CHUNKS + chunk, h, w * block : (w + 1) * block]
                    e = right[(2 * b + 1) * CHUNKS + chunk, h, w * block : (w + 1) * block]
                    col_sum[b, n] = c + e
                    col_diff[b, n] = c - e
            for a in range(3):
                for h in range(2):
                    row_sum[a, h] = left[2 * a * CHUNKS + chunk, h] + left[(2 * a + 1) * CHUNKS + chunk, h]
            for a in range(3):
                one, two, three = {}, {}, {}
                for n, (h, w) in enumerate(windows):
                    c = [right[2 * b * CHUNKS + chunk, h, w * block : (w + 1) * block] for b in range(3)]
                    plus = [col_sum[b, n] for b in range(3)]
                    minus = [col_diff[b, n] for b in range(3)]
                    for s in range(half):
                        r = w * half + s
                        p = jnp.broadcast_to(left[2 * a * CHUNKS + chunk, h, r : r + 1], (block, LANES))
                        q = jnp.broadcast_to(left[(2 * a + 1) * CHUNKS + chunk, h, r : r + 1], (block, LANES))
                        pq = jnp.broadcast_to(row_sum[a, h, r : r + 1], (block, LANES))
                        for b in range(3):
                            x, y, z = pq * c[b], p * plus[b], q * minus[b]
                            one[s, b] = x if n == 0 else one[s, b] + x
                            two[s, b] = y if n == 0 else two[s, b] + y
                            three[s, b] = z if n == 0 else three[s, b] + z
                for pair in range(half // 2):
                    for b in range(3):
                        keys = [(2 * pair, b), (2 * pair + 1, b)]
                        re = jnp.concatenate([one[k] - three[k] for k in keys], 0).astype(jnp.bfloat16)
                        im = jnp.concatenate([one[k] - two[k] for k in keys], 0).astype(jnp.bfloat16)
                        first = ((pair * 3 + a) * 3 + b) * 2 * block
                        cross[into, first : first + 2 * block, :LANES] = re
                        cross[into, first : first + 2 * block, LANES:] = im

        def one_chunk(chunk, carry):
            products(chunk, chunk)
            return carry

        lax.fori_loop(0, CHUNKS, one_chunk, 0)
        fetch.wait()
        copies = []
        for n in range(LAG // TILE):
            acc = None
            for chunk in range(CHUNKS):
                new = jnp.dot(
                    cross[chunk],
                    table_ref[2 * LANES * chunk : 2 * LANES * (chunk + 1), n * TILE : (n + 1) * TILE],
                    preferred_element_type=jnp.float32,
                )
                acc = new if acc is None else acc + new
            for s in range(half):
                inv = inv_ref[s][:, :1]
                for c in range(9):
                    group = ((s // 2) * 9 + c) * 2 + s % 2
                    staged[n, s, c] = acc[group * block : (group + 1) * block] * inv
            copies.append(pltpu.make_async_copy(staged.at[n], out_hbm.at[:, :, :, pl.ds(n * TILE, TILE)], out_sem.at[n]))
            copies[-1].start()
        for copy in copies:
            copy.wait()

    return kernel


def masks(usable, half, block, span):
    def kernel(usable_ref, rmask, cmask, inv_ref):
        row, col, win = (lax.axis_index(a) for a in AXES)
        usable = usable_ref[...].astype(jnp.float32)
        stations = usable.shape[1]

        def column(first, count, h):
            rows = jnp.concatenate(
                [jnp.broadcast_to(usable[w : w + 1], (count, stations)) for w in range(h * span, (h + 1) * span)], 0
            )
            shape = (span * count, stations)
            picked = lax.broadcasted_iota(jnp.int32, shape, 1) == first + lax.broadcasted_iota(jnp.int32, shape, 0) % count
            return jnp.sum(jnp.where(picked, rows, 0.0), 1, keepdims=True)

        counts = [jnp.zeros((block, LANES), jnp.float32) for _ in range(half)]
        for h in range(2):
            rm = jnp.broadcast_to(column(row * block + win * half, half, h), (span * half, LANES))
            cm = jnp.broadcast_to(column(col * block, block, h), (span * block, LANES))
            rmask[h] = rm
            cmask[h] = cm
            for w in range(span):
                for s in range(half):
                    counts[s] = counts[s] + rm[w * half + s : w * half + s + 1] * cm[w * block : (w + 1) * block]
        for s in range(half):
            inv_ref[s] = 1.0 / jnp.maximum(counts[s], 1.0)

    in_vmem = pl.BlockSpec(memory_space=pltpu.VMEM)
    shapes = ((2, span * half, LANES), (2, span * block, LANES), (half, block, LANES))
    return pl.pallas_call(
        kernel,
        out_shape=tuple(jax.ShapeDtypeStruct(shape, jnp.float32) for shape in shapes),
        in_specs=[in_vmem],
        out_specs=(in_vmem,) * 3,
        cost_estimate=pl.CostEstimate(flops=10**10, bytes_accessed=2**20, transcendentals=0),
        compiler_params=pltpu.CompilerParams(vmem_limit_bytes=4 * 1024 * 1024),
    )(usable)


def correlate(rows, cols, flags, table, row_places, col_places, half, block, span):
    groups = half * 9 * block
    pieces = 6 * CHUNKS
    slots = len(rows) + len(cols) + 3
    hbm = pl.BlockSpec(memory_space=pltpu.HBM)
    return pl.pallas_call(
        make_kernel(row_places, col_places, half, block, span),
        out_shape=jax.ShapeDtypeStruct((half, 9, block, LAG), jnp.float32),
        in_specs=[pl.BlockSpec(memory_space=pltpu.VMEM)] * slots + [hbm],
        out_specs=hbm,
        scratch_shapes=[
            pltpu.VMEM((pieces, 2, span * half, LANES), jnp.float32),
            pltpu.VMEM((pieces, 2, span * block, LANES), jnp.float32),
            pltpu.VMEM((CHUNKS, groups, 2 * LANES), jnp.bfloat16),
            pltpu.VMEM((3, 2 * span, block, LANES), jnp.float32),
            pltpu.VMEM((3, 2 * span, block, LANES), jnp.float32),
            pltpu.VMEM((3, 2, span * half, LANES), jnp.float32),
            pltpu.VMEM((LAG // TILE, half, 9, block, TILE), jnp.float32),
            pltpu.SemaphoreType.DMA((LAG // TILE,)),
            pltpu.VMEM(table.shape, jnp.bfloat16),
            pltpu.SemaphoreType.DMA,
        ],
        compiler_params=pltpu.CompilerParams(vmem_limit_bytes=52 * 1024 * 1024),
    )(*rows, *cols, *flags, table)


def split_stations(spectra, half):
    span, block, shard = spectra.shape

    def kernel(spectra_ref, theirs_ref, mine_ref):
        low = [spectra_ref[w, :half] for w in range(span)]
        high = [spectra_ref[w, half:] for w in range(span)]
        first = lax.axis_index("win") == 0
        low, high = jnp.concatenate(low, 0), jnp.concatenate(high, 0)
        theirs_ref[...] = jnp.where(first, high, low)
        mine_ref[: span * half] = jnp.where(first, low, high)
        mine_ref[span * half :] = jnp.zeros((span * half, shard), jnp.bfloat16)

    in_vmem = pl.BlockSpec(memory_space=pltpu.VMEM)
    return pl.pallas_call(
        kernel,
        out_shape=(
            jax.ShapeDtypeStruct((span * half, shard), jnp.bfloat16),
            jax.ShapeDtypeStruct((2 * span * half, shard), jnp.bfloat16),
        ),
        in_specs=[in_vmem],
        out_specs=(in_vmem, in_vmem),
        compiler_params=pltpu.CompilerParams(vmem_limit_bytes=4 * 1024 * 1024),
    )(spectra)


def body(spectra, usable):
    span, block, shard = spectra.shape
    n_row, n_col, n_win = (lax.axis_size(a) for a in AXES)
    assert n_row == n_col and n_win == 2
    half = block // n_win

    def send(data, move):
        pairs = []
        for r in range(n_row):
            for c in range(n_col):
                for w in range(n_win):
                    r2, c2, w2 = move(r, c, w)
                    pairs.append(((r * n_col + c) * n_win + w, (r2 * n_col + c2) * n_win + w2))
        return lax.ppermute(data, AXES, pairs)

    def other_win(r, c, w):
        return r, c, 1 - w

    flat = spectra.reshape(span * block, shard)
    turned = send(flat, lambda r, c, w: (n_row - 1 - c, r, w))
    theirs, mine = split_stations(spectra, half)
    got = send(theirs, other_win)
    flags = masks(usable, half, block, span)
    mine, *flags = lax.optimization_barrier((mine, *flags))
    mine = lax.dynamic_update_slice(mine, got, (span * half, 0))

    if n_row == 4:
        across = send(mine, lambda r, c, w: (r, c ^ 3, w))
        beside = send(mine, lambda r, c, w: (r, c ^ 1, w))
        shifted = [across, beside, send(across, lambda r, c, w: (r, c ^ 1, w))]
        rows = [mine] + shifted
        row_places = [lambda r, c, w, k=k: c ^ k for k in (0, 3, 1, 2)]
        near = [
            turned,
            send(turned, lambda r, c, w: (r ^ 2, c, w)),
            send(turned, other_win),
            send(turned, lambda r, c, w: (r ^ 2, c, 1 - w)),
        ]
        last = lax.optimization_barrier((near[3], *shifted))[0]
        cols = near + [send(x, lambda r, c, w: (r ^ 1, c, w)) for x in near[:3] + [last]]
        col_places = [
            lambda r, c, w, e=e, d=d: (n_row - 1 - (r ^ e), w ^ d)
            for e, d in ((0, 0), (2, 0), (0, 1), (2, 1), (1, 0), (3, 0), (1, 1), (3, 1))
        ]
    else:
        gathered = lax.all_gather(mine, "col", axis=0)
        rows = [gathered[i] for i in range(n_col)]
        row_places = [lambda r, c, w, i=i: i for i in range(n_col)]
        near = lax.all_gather(turned, "row", axis=0)
        far = send(near, other_win)
        cols = [x[i] for x in (near, far) for i in range(n_row)]
        col_places = [lambda r, c, w, i=i, d=d: (n_row - 1 - i, w ^ d) for d in range(2) for i in range(n_row)]

    out = correlate(rows, cols, flags, jnp.asarray(build_table()), row_places, col_places, half, block, span)
    return out.transpose(0, 2, 1, 3)


def solution(mesh):
    placed = (P("win", "row", "col"), P())
    return jax.shard_map(
        body,
        mesh=mesh,
        in_specs=placed,
        out_specs=P(("row", "win"), "col", None, None),
        check_vma=False,
    )
```

```python
import math

import jax
import jax.numpy as jnp
import numpy as np
from jax import lax
from jax.experimental import pallas as pl
from jax.experimental.pallas import tpu as pltpu
from jax.sharding import PartitionSpec as P

F = 1024
LAG = 768
DEC = 2
LANES = 128
CHUNKS = F // LANES
TILE = 256
FIRST_FLOPS = 10**9
AXES = ("row", "col", "win")


def build_table():
    shift = DEC * (np.arange(LAG, dtype=np.int64) - LAG // 2)
    phase = (np.arange(F, dtype=np.int64)[:, None] * shift[None, :]) % (2 * F)
    angle = phase.astype(np.float64) * (math.pi / F)
    scale = 1.0 / math.sqrt(F)
    both = np.stack([np.cos(angle) * scale, -np.sin(angle) * scale])
    both = both.reshape(2, CHUNKS, LANES, LAG).transpose(1, 0, 2, 3)
    return both.reshape(2 * F, LAG).astype(np.float32).astype(jnp.bfloat16)


def half_products(second, row_slots, col_slots, row_places, col_places, rmask, cmask, scratch, half, block, span, emit):
    left, right, col_sum, col_diff, row_sum = scratch
    at = tuple(lax.axis_index(name) for name in AXES)
    own = 1 - at[2] if second else at[2]
    per_shard = row_slots[0].shape[1] // LANES
    first_row = span * half if second else 0

    mask = rmask[own]
    for ref, place in zip(row_slots, row_places):
        shard = place(*at)
        for i in range(per_shard):
            data = ref[first_row : first_row + span * half, i * LANES : (i + 1) * LANES]
            left[shard * per_shard + i] = data.astype(jnp.float32) * mask
    mask = cmask[own]
    for ref, place in zip(col_slots, col_places):
        shard = place(*at)
        for i in range(per_shard):
            right[shard * per_shard + i] = ref[:, i * LANES : (i + 1) * LANES].astype(jnp.float32) * mask

    def one_chunk(chunk, carry):
        for b in range(3):
            c, e = right[2 * b * CHUNKS + chunk], right[(2 * b + 1) * CHUNKS + chunk]
            col_sum[b] = c + e
            col_diff[b] = c - e
        for a in range(3):
            row_sum[a] = left[2 * a * CHUNKS + chunk] + left[(2 * a + 1) * CHUNKS + chunk]
        for a in range(3):
            one, two, three = {}, {}, {}
            for w in range(span):
                rows = slice(w * block, (w + 1) * block)
                c = [right[2 * b * CHUNKS + chunk, rows] for b in range(3)]
                plus = [col_sum[b, rows] for b in range(3)]
                minus = [col_diff[b, rows] for b in range(3)]
                for s in range(half):
                    r = w * half + s
                    p = jnp.broadcast_to(left[2 * a * CHUNKS + chunk, r : r + 1], (block, LANES))
                    q = jnp.broadcast_to(left[(2 * a + 1) * CHUNKS + chunk, r : r + 1], (block, LANES))
                    pq = jnp.broadcast_to(row_sum[a, r : r + 1], (block, LANES))
                    for b in range(3):
                        x, y, z = pq * c[b], p * plus[b], q * minus[b]
                        one[s, b] = x if w == 0 else one[s, b] + x
                        two[s, b] = y if w == 0 else two[s, b] + y
                        three[s, b] = z if w == 0 else three[s, b] + z
            for pair in range(half // 2):
                for b in range(3):
                    keys = [(2 * pair, b), (2 * pair + 1, b)]
                    first = ((pair * 3 + a) * 3 + b) * 2 * block
                    emit(chunk, first, [one[k] - three[k] for k in keys], [one[k] - two[k] for k in keys])
        return carry

    lax.fori_loop(0, CHUNKS, one_chunk, 0)


def half_scratch(half, block, span):
    pieces = 6 * CHUNKS
    return [
        pltpu.VMEM((pieces, span * half, LANES), jnp.float32),
        pltpu.VMEM((pieces, span * block, LANES), jnp.float32),
        pltpu.VMEM((3, span * block, LANES), jnp.float32),
        pltpu.VMEM((3, span * block, LANES), jnp.float32),
        pltpu.VMEM((3, span * half, LANES), jnp.float32),
    ]


def first_half(rows, cols, rmask, cmask, row_places, col_places, half, block, span):
    n_rows, n_cols = len(rows), len(cols)
    groups = half * 9 * block

    def kernel(*refs):
        row_slots, col_slots = refs[:n_rows], refs[n_rows : n_rows + n_cols]
        rmask, cmask, real_ref, imag_ref, *scratch = refs[n_rows + n_cols :]

        def emit(chunk, first, reals, imags):
            for n in range(2):
                real_ref[chunk, first + n * block : first + (n + 1) * block] = reals[n]
                imag_ref[chunk, first + n * block : first + (n + 1) * block] = imags[n]

        half_products(
            False, row_slots, col_slots, row_places, col_places, rmask, cmask, scratch, half, block, span, emit
        )

    in_vmem = pl.BlockSpec(memory_space=pltpu.VMEM)
    return pl.pallas_call(
        kernel,
        out_shape=(jax.ShapeDtypeStruct((CHUNKS, groups, LANES), jnp.float32),) * 2,
        in_specs=[in_vmem] * (n_rows + n_cols + 2),
        out_specs=(in_vmem,) * 2,
        scratch_shapes=half_scratch(half, block, span),
        cost_estimate=pl.CostEstimate(flops=FIRST_FLOPS, bytes_accessed=2**20, transcendentals=0),
        compiler_params=pltpu.CompilerParams(vmem_limit_bytes=32 * 1024 * 1024),
    )(*rows, *cols, rmask, cmask)


def correlate(rows, cols, parts, flags, table, row_places, col_places, half, block, span):
    n_rows, n_cols = len(rows), len(cols)
    groups = half * 9 * block

    def kernel(*refs):
        row_slots, col_slots = refs[:n_rows], refs[n_rows : n_rows + n_cols]
        real_ref, imag_ref, rmask, cmask, inv_ref, table_ref, out_hbm, *scratch = refs[n_rows + n_cols :]
        *scratch, cross, staged, out_sem = scratch

        def emit(chunk, first, reals, imags):
            rows = slice(first, first + 2 * block)
            re = real_ref[chunk, rows] + jnp.concatenate(reals, 0)
            im = imag_ref[chunk, rows] + jnp.concatenate(imags, 0)
            cross[chunk, rows, :LANES] = re.astype(jnp.bfloat16)
            cross[chunk, rows, LANES:] = im.astype(jnp.bfloat16)

        half_products(
            True, row_slots, col_slots, row_places, col_places, rmask, cmask, scratch, half, block, span, emit
        )
        copies = []
        for n in range(LAG // TILE):
            acc = None
            for chunk in range(CHUNKS):
                new = jnp.dot(
                    cross[chunk],
                    table_ref[2 * LANES * chunk : 2 * LANES * (chunk + 1), n * TILE : (n + 1) * TILE],
                    preferred_element_type=jnp.float32,
                )
                acc = new if acc is None else acc + new
            for s in range(half):
                inv = inv_ref[s][:, :1]
                for c in range(9):
                    group = ((s // 2) * 9 + c) * 2 + s % 2
                    staged[n, s, c] = acc[group * block : (group + 1) * block] * inv
            copies.append(pltpu.make_async_copy(staged.at[n], out_hbm.at[:, :, :, pl.ds(n * TILE, TILE)], out_sem.at[n]))
            copies[-1].start()
        for copy in copies:
            copy.wait()

    return pl.pallas_call(
        kernel,
        out_shape=jax.ShapeDtypeStruct((half, 9, block, LAG), jnp.float32),
        in_specs=[pl.BlockSpec(memory_space=pltpu.VMEM)] * (n_rows + n_cols + 6),
        out_specs=pl.BlockSpec(memory_space=pltpu.HBM),
        scratch_shapes=half_scratch(half, block, span)
        + [
            pltpu.VMEM((CHUNKS, groups, 2 * LANES), jnp.bfloat16),
            pltpu.VMEM((LAG // TILE, half, 9, block, TILE), jnp.float32),
            pltpu.SemaphoreType.DMA((LAG // TILE,)),
        ],
        compiler_params=pltpu.CompilerParams(vmem_limit_bytes=40 * 1024 * 1024),
    )(*rows, *cols, *parts, *flags, table)


def masks(usable, half, block, span):
    def kernel(usable_ref, rmask, cmask, inv_ref):
        row, col, win = (lax.axis_index(a) for a in AXES)
        usable = usable_ref[...].astype(jnp.float32)
        stations = usable.shape[1]

        def column(first, count, h):
            rows = jnp.concatenate(
                [jnp.broadcast_to(usable[w : w + 1], (count, stations)) for w in range(h * span, (h + 1) * span)], 0
            )
            shape = (span * count, stations)
            picked = lax.broadcasted_iota(jnp.int32, shape, 1) == first + lax.broadcasted_iota(jnp.int32, shape, 0) % count
            return jnp.sum(jnp.where(picked, rows, 0.0), 1, keepdims=True)

        counts = [jnp.zeros((block, LANES), jnp.float32) for _ in range(half)]
        for h in range(2):
            rm = jnp.broadcast_to(column(row * block + win * half, half, h), (span * half, LANES))
            cm = jnp.broadcast_to(column(col * block, block, h), (span * block, LANES))
            rmask[h] = rm
            cmask[h] = cm
            for w in range(span):
                for s in range(half):
                    counts[s] = counts[s] + rm[w * half + s : w * half + s + 1] * cm[w * block : (w + 1) * block]
        for s in range(half):
            inv_ref[s] = 1.0 / jnp.maximum(counts[s], 1.0)

    in_vmem = pl.BlockSpec(memory_space=pltpu.VMEM)
    shapes = ((2, span * half, LANES), (2, span * block, LANES), (half, block, LANES))
    return pl.pallas_call(
        kernel,
        out_shape=tuple(jax.ShapeDtypeStruct(shape, jnp.float32) for shape in shapes),
        in_specs=[in_vmem],
        out_specs=(in_vmem,) * 3,
        cost_estimate=pl.CostEstimate(flops=10**10, bytes_accessed=2**20, transcendentals=0),
        compiler_params=pltpu.CompilerParams(vmem_limit_bytes=4 * 1024 * 1024),
    )(usable)


def split_stations(spectra, half):
    span, block, shard = spectra.shape

    def kernel(spectra_ref, theirs_ref, mine_ref):
        low = [spectra_ref[w, :half] for w in range(span)]
        high = [spectra_ref[w, half:] for w in range(span)]
        first = lax.axis_index("win") == 0
        low, high = jnp.concatenate(low, 0), jnp.concatenate(high, 0)
        theirs_ref[...] = jnp.where(first, high, low)
        mine_ref[: span * half] = jnp.where(first, low, high)
        mine_ref[span * half :] = jnp.zeros((span * half, shard), jnp.bfloat16)

    in_vmem = pl.BlockSpec(memory_space=pltpu.VMEM)
    return pl.pallas_call(
        kernel,
        out_shape=(
            jax.ShapeDtypeStruct((span * half, shard), jnp.bfloat16),
            jax.ShapeDtypeStruct((2 * span * half, shard), jnp.bfloat16),
        ),
        in_specs=[in_vmem],
        out_specs=(in_vmem, in_vmem),
        compiler_params=pltpu.CompilerParams(vmem_limit_bytes=4 * 1024 * 1024),
    )(spectra)


def body(spectra, usable):
    span, block, shard = spectra.shape
    n_row, n_col, n_win = (lax.axis_size(a) for a in AXES)
    assert n_row == n_col and n_win == 2
    half = block // n_win

    def send(data, move):
        pairs = []
        for r in range(n_row):
            for c in range(n_col):
                for w in range(n_win):
                    r2, c2, w2 = move(r, c, w)
                    pairs.append(((r * n_col + c) * n_win + w, (r2 * n_col + c2) * n_win + w2))
        return lax.ppermute(data, AXES, pairs)

    def other_win(r, c, w):
        return r, c, 1 - w

    flat = spectra.reshape(span * block, shard)
    turned = send(flat, lambda r, c, w: (n_row - 1 - c, r, w))
    theirs, mine = split_stations(spectra, half)
    got = send(theirs, other_win)
    flags = masks(usable, half, block, span)
    mine, *flags = lax.optimization_barrier((mine, *flags))
    mine = lax.dynamic_update_slice(mine, got, (span * half, 0))

    if n_row == 4:
        across = send(mine, lambda r, c, w: (r, c ^ 3, w))
        beside = send(mine, lambda r, c, w: (r, c ^ 1, w))
        shifted = [across, beside, send(across, lambda r, c, w: (r, c ^ 1, w))]
        rows = [mine] + shifted
        row_places = [lambda r, c, w, k=k: c ^ k for k in (0, 3, 1, 2)]
        near = [
            turned,
            send(turned, lambda r, c, w: (r ^ 2, c, w)),
            send(turned, other_win),
            send(turned, lambda r, c, w: (r ^ 2, c, 1 - w)),
        ]
        last = lax.optimization_barrier((near[3], *shifted))[0]
        swapped = [send(x, lambda r, c, w: (r ^ 1, c, w)) for x in near[:3] + [last]]
        cols = [[*near[:2], *swapped[:2]], [*near[2:], *swapped[2:]]]
        col_places = [lambda r, c, w, e=e: n_row - 1 - (r ^ e) for e in (0, 2, 1, 3)]
    else:
        gathered = lax.all_gather(mine, "col", axis=0)
        rows = [gathered[i] for i in range(n_col)]
        row_places = [lambda r, c, w, i=i: i for i in range(n_col)]
        near = lax.all_gather(turned, "row", axis=0)
        far = send(near, other_win)
        cols = [[x[i] for i in range(n_row)] for x in (near, far)]
        col_places = [lambda r, c, w, i=i: n_row - 1 - i for i in range(n_row)]

    parts = first_half(rows, cols[0], *flags[:2], row_places, col_places, half, block, span)
    out = correlate(
        rows, cols[1], parts, flags, jnp.asarray(build_table()), row_places, col_places, half, block, span
    )
    return out.transpose(0, 2, 1, 3)


def solution(mesh):
    placed = (P("win", "row", "col"), P())
    return jax.shard_map(
        body,
        mesh=mesh,
        in_specs=placed,
        out_specs=P(("row", "win"), "col", None, None),
        check_vma=False,
    )
```

```python
import math

import jax
import jax.numpy as jnp
import numpy as np
from jax import lax
from jax.experimental import pallas as pl
from jax.experimental.pallas import tpu as pltpu
from jax.sharding import PartitionSpec as P

F = 1024
LAG = 768
DEC = 2
LANES = 128
CHUNKS = F // LANES
TILE = 256
FIRST_FLOPS = 10**9
AXES = ("row", "col", "win")


def build_table():
    shift = DEC * (np.arange(LAG, dtype=np.int64) - LAG // 2)
    phase = (np.arange(F, dtype=np.int64)[:, None] * shift[None, :]) % (2 * F)
    angle = phase.astype(np.float64) * (math.pi / F)
    scale = 1.0 / math.sqrt(F)
    both = np.stack([np.cos(angle) * scale, -np.sin(angle) * scale])
    both = both.reshape(2, CHUNKS, LANES, LAG).transpose(1, 0, 2, 3)
    return both.reshape(2 * F, LAG).astype(np.float32).astype(jnp.bfloat16)


def half_products(second, row_slots, col_slots, row_places, col_places, rmask, cmask, scratch, half, block, span, emit):
    left, right, col_sum, col_diff, row_sum = scratch
    at = tuple(lax.axis_index(name) for name in AXES)
    own = 1 - at[2] if second else at[2]
    per_shard = row_slots[0].shape[1] // LANES
    first_row = span * half if second else 0

    mask = rmask[own]
    for ref, place in zip(row_slots, row_places):
        shard = place(*at)
        for i in range(per_shard):
            data = ref[first_row : first_row + span * half, i * LANES : (i + 1) * LANES]
            left[shard * per_shard + i] = data.astype(jnp.float32) * mask
    mask = cmask[own]
    for ref, place in zip(col_slots, col_places):
        shard = place(*at)
        for i in range(per_shard):
            right[shard * per_shard + i] = ref[:, i * LANES : (i + 1) * LANES].astype(jnp.float32) * mask

    def one_chunk(chunk, carry):
        for b in range(3):
            c, e = right[2 * b * CHUNKS + chunk], right[(2 * b + 1) * CHUNKS + chunk]
            col_sum[b] = c + e
            col_diff[b] = c - e
        for a in range(3):
            row_sum[a] = left[2 * a * CHUNKS + chunk] + left[(2 * a + 1) * CHUNKS + chunk]
        for a in range(3):
            one, two, three = {}, {}, {}
            for w in range(span):
                rows = slice(w * block, (w + 1) * block)
                c = [right[2 * b * CHUNKS + chunk, rows] for b in range(3)]
                plus = [col_sum[b, rows] for b in range(3)]
                minus = [col_diff[b, rows] for b in range(3)]
                for s in range(half):
                    r = w * half + s
                    p = jnp.broadcast_to(left[2 * a * CHUNKS + chunk, r : r + 1], (block, LANES))
                    q = jnp.broadcast_to(left[(2 * a + 1) * CHUNKS + chunk, r : r + 1], (block, LANES))
                    pq = jnp.broadcast_to(row_sum[a, r : r + 1], (block, LANES))
                    for b in range(3):
                        x, y, z = pq * c[b], p * plus[b], q * minus[b]
                        one[s, b] = x if w == 0 else one[s, b] + x
                        two[s, b] = y if w == 0 else two[s, b] + y
                        three[s, b] = z if w == 0 else three[s, b] + z
            for pair in range(half // 2):
                for b in range(3):
                    keys = [(2 * pair, b), (2 * pair + 1, b)]
                    first = ((pair * 3 + a) * 3 + b) * 2 * block
                    emit(chunk, first, [one[k] - three[k] for k in keys], [one[k] - two[k] for k in keys])
        return carry

    lax.fori_loop(0, CHUNKS, one_chunk, 0)


def half_scratch(half, block, span):
    pieces = 6 * CHUNKS
    return [
        pltpu.VMEM((pieces, span * half, LANES), jnp.float32),
        pltpu.VMEM((pieces, span * block, LANES), jnp.float32),
        pltpu.VMEM((3, span * block, LANES), jnp.float32),
        pltpu.VMEM((3, span * block, LANES), jnp.float32),
        pltpu.VMEM((3, span * half, LANES), jnp.float32),
    ]


def first_half(rows, cols, rmask, cmask, row_places, col_places, half, block, span):
    n_rows, n_cols = len(rows), len(cols)
    groups = half * 9 * block

    def kernel(*refs):
        row_slots, col_slots = refs[:n_rows], refs[n_rows : n_rows + n_cols]
        rmask, cmask, real_ref, imag_ref, *scratch = refs[n_rows + n_cols :]

        def emit(chunk, first, reals, imags):
            for n in range(2):
                real_ref[chunk, first + n * block : first + (n + 1) * block] = reals[n]
                imag_ref[chunk, first + n * block : first + (n + 1) * block] = imags[n]

        half_products(
            False, row_slots, col_slots, row_places, col_places, rmask, cmask, scratch, half, block, span, emit
        )

    in_vmem = pl.BlockSpec(memory_space=pltpu.VMEM)
    return pl.pallas_call(
        kernel,
        out_shape=(jax.ShapeDtypeStruct((CHUNKS, groups, LANES), jnp.float32),) * 2,
        in_specs=[in_vmem] * (n_rows + n_cols + 2),
        out_specs=(in_vmem,) * 2,
        scratch_shapes=half_scratch(half, block, span),
        cost_estimate=pl.CostEstimate(flops=FIRST_FLOPS, bytes_accessed=2**20, transcendentals=0),
        compiler_params=pltpu.CompilerParams(vmem_limit_bytes=32 * 1024 * 1024),
    )(*rows, *cols, rmask, cmask)


def correlate(rows, cols, parts, flags, table, row_places, col_places, half, block, span):
    n_rows, n_cols = len(rows), len(cols)
    groups = half * 9 * block

    def kernel(*refs):
        row_slots, col_slots = refs[:n_rows], refs[n_rows : n_rows + n_cols]
        real_ref, imag_ref, rmask, cmask, inv_ref, table_ref, out_hbm, *scratch = refs[n_rows + n_cols :]
        *scratch, cross, staged, out_sem = scratch

        def emit(chunk, first, reals, imags):
            rows = slice(first, first + 2 * block)
            re = real_ref[chunk, rows] + jnp.concatenate(reals, 0)
            im = imag_ref[chunk, rows] + jnp.concatenate(imags, 0)
            cross[chunk, rows, :LANES] = re.astype(jnp.bfloat16)
            cross[chunk, rows, LANES:] = im.astype(jnp.bfloat16)

        half_products(
            True, row_slots, col_slots, row_places, col_places, rmask, cmask, scratch, half, block, span, emit
        )
        copies = []
        for n in range(LAG // TILE):
            acc = None
            for chunk in range(CHUNKS):
                new = jnp.dot(
                    cross[chunk],
                    table_ref[2 * LANES * chunk : 2 * LANES * (chunk + 1), n * TILE : (n + 1) * TILE],
                    preferred_element_type=jnp.float32,
                )
                acc = new if acc is None else acc + new
            for s in range(half):
                inv = inv_ref[s][:, :1]
                for c in range(9):
                    group = ((s // 2) * 9 + c) * 2 + s % 2
                    staged[n, s, c] = acc[group * block : (group + 1) * block] * inv
            copies.append(pltpu.make_async_copy(staged.at[n], out_hbm.at[:, :, :, pl.ds(n * TILE, TILE)], out_sem.at[n]))
            copies[-1].start()
        for copy in copies:
            copy.wait()

    return pl.pallas_call(
        kernel,
        out_shape=jax.ShapeDtypeStruct((half, 9, block, LAG), jnp.float32),
        in_specs=[pl.BlockSpec(memory_space=pltpu.VMEM)] * (n_rows + n_cols + 6),
        out_specs=pl.BlockSpec(memory_space=pltpu.HBM),
        scratch_shapes=half_scratch(half, block, span)
        + [
            pltpu.VMEM((CHUNKS, groups, 2 * LANES), jnp.bfloat16),
            pltpu.VMEM((LAG // TILE, half, 9, block, TILE), jnp.float32),
            pltpu.SemaphoreType.DMA((LAG // TILE,)),
        ],
        compiler_params=pltpu.CompilerParams(vmem_limit_bytes=40 * 1024 * 1024),
    )(*rows, *cols, *parts, *flags, table)


def masks(usable, half, block, span):
    def kernel(usable_ref, rmask, cmask, inv_ref):
        row, col, win = (lax.axis_index(a) for a in AXES)
        usable = usable_ref[...].astype(jnp.float32)
        stations = usable.shape[1]

        def column(first, count, h):
            rows = jnp.concatenate(
                [jnp.broadcast_to(usable[w : w + 1], (count, stations)) for w in range(h * span, (h + 1) * span)], 0
            )
            shape = (span * count, stations)
            picked = lax.broadcasted_iota(jnp.int32, shape, 1) == first + lax.broadcasted_iota(jnp.int32, shape, 0) % count
            return jnp.sum(jnp.where(picked, rows, 0.0), 1, keepdims=True)

        counts = [jnp.zeros((block, LANES), jnp.float32) for _ in range(half)]
        for h in range(2):
            rm = jnp.broadcast_to(column(row * block + win * half, half, h), (span * half, LANES))
            cm = jnp.broadcast_to(column(col * block, block, h), (span * block, LANES))
            rmask[h] = rm
            cmask[h] = cm
            for w in range(span):
                for s in range(half):
                    counts[s] = counts[s] + rm[w * half + s : w * half + s + 1] * cm[w * block : (w + 1) * block]
        for s in range(half):
            inv_ref[s] = 1.0 / jnp.maximum(counts[s], 1.0)

    in_vmem = pl.BlockSpec(memory_space=pltpu.VMEM)
    shapes = ((2, span * half, LANES), (2, span * block, LANES), (half, block, LANES))
    return pl.pallas_call(
        kernel,
        out_shape=tuple(jax.ShapeDtypeStruct(shape, jnp.float32) for shape in shapes),
        in_specs=[in_vmem],
        out_specs=(in_vmem,) * 3,
        cost_estimate=pl.CostEstimate(flops=10**10, bytes_accessed=2**20, transcendentals=0),
        compiler_params=pltpu.CompilerParams(vmem_limit_bytes=4 * 1024 * 1024),
    )(usable)


def split_stations(spectra, half):
    span, block, shard = spectra.shape

    def kernel(spectra_ref, theirs_ref, mine_ref):
        low = [spectra_ref[w, :half] for w in range(span)]
        high = [spectra_ref[w, half:] for w in range(span)]
        first = lax.axis_index("win") == 0
        low, high = jnp.concatenate(low, 0), jnp.concatenate(high, 0)
        theirs_ref[...] = jnp.where(first, high, low)
        mine_ref[: span * half] = jnp.where(first, low, high)
        mine_ref[span * half :] = jnp.zeros((span * half, shard), jnp.bfloat16)

    in_vmem = pl.BlockSpec(memory_space=pltpu.VMEM)
    return pl.pallas_call(
        kernel,
        out_shape=(
            jax.ShapeDtypeStruct((span * half, shard), jnp.bfloat16),
            jax.ShapeDtypeStruct((2 * span * half, shard), jnp.bfloat16),
        ),
        in_specs=[in_vmem],
        out_specs=(in_vmem, in_vmem),
        compiler_params=pltpu.CompilerParams(vmem_limit_bytes=4 * 1024 * 1024),
    )(spectra)


def body(spectra, usable):
    span, block, shard = spectra.shape
    n_row, n_col, n_win = (lax.axis_size(a) for a in AXES)
    assert n_row == n_col and n_win == 2
    half = block // n_win

    def send(data, move):
        pairs = []
        for r in range(n_row):
            for c in range(n_col):
                for w in range(n_win):
                    r2, c2, w2 = move(r, c, w)
                    pairs.append(((r * n_col + c) * n_win + w, (r2 * n_col + c2) * n_win + w2))
        return lax.ppermute(data, AXES, pairs)

    def other_win(r, c, w):
        return r, c, 1 - w

    flat = spectra.reshape(span * block, shard)
    turned = send(flat, lambda r, c, w: (n_row - 1 - c, r, w))
    theirs, mine = split_stations(spectra, half)
    got = send(theirs, other_win)
    flags = masks(usable, half, block, span)
    mine, *flags = lax.optimization_barrier((mine, *flags))
    mine = lax.dynamic_update_slice(mine, got, (span * half, 0))

    if n_row == 4:
        across = send(mine, lambda r, c, w: (r, c ^ 3, w))
        ready = lax.optimization_barrier((mine, turned))[0]
        beside = send(ready, lambda r, c, w: (r, c ^ 1, w))
        shifted = [across, beside, send(across, lambda r, c, w: (r, c ^ 1, w))]
        rows = [mine] + shifted
        row_places = [lambda r, c, w, k=k: c ^ k for k in (0, 3, 1, 2)]
        near = [
            turned,
            send(turned, lambda r, c, w: (r ^ 2, c, w)),
            send(turned, other_win),
            send(turned, lambda r, c, w: (r ^ 2, c, 1 - w)),
        ]
        last = lax.optimization_barrier((near[3], *shifted))[0]
        swapped = [send(x, lambda r, c, w: (r ^ 1, c, w)) for x in near[:3] + [last]]
        cols = [[*near[:2], *swapped[:2]], [*near[2:], *swapped[2:]]]
        col_places = [lambda r, c, w, e=e: n_row - 1 - (r ^ e) for e in (0, 2, 1, 3)]
    else:
        gathered = lax.all_gather(mine, "col", axis=0)
        rows = [gathered[i] for i in range(n_col)]
        row_places = [lambda r, c, w, i=i: i for i in range(n_col)]
        near = lax.all_gather(turned, "row", axis=0)
        far = send(near, other_win)
        cols = [[x[i] for i in range(n_row)] for x in (near, far)]
        col_places = [lambda r, c, w, i=i: n_row - 1 - i for i in range(n_row)]

    parts = first_half(rows, cols[0], *flags[:2], row_places, col_places, half, block, span)
    out = correlate(
        rows, cols[1], parts, flags, jnp.asarray(build_table()), row_places, col_places, half, block, span
    )
    return out.transpose(0, 2, 1, 3)


def solution(mesh):
    placed = (P("win", "row", "col"), P())
    return jax.shard_map(
        body,
        mesh=mesh,
        in_specs=placed,
        out_specs=P(("row", "win"), "col", None, None),
        check_vma=False,
    )
```

```python
import math

import jax
import jax.numpy as jnp
import numpy as np
from jax import lax
from jax.experimental import pallas as pl
from jax.experimental.pallas import tpu as pltpu
from jax.sharding import PartitionSpec as P

F = 1024
LAG = 768
DEC = 2
LANES = 128
CHUNKS = F // LANES
TILE = 256
FIRST_FLOPS = 10**9
AXES = ("row", "col", "win")


def build_table():
    shift = DEC * (np.arange(LAG, dtype=np.int64) - LAG // 2)
    phase = (np.arange(F, dtype=np.int64)[:, None] * shift[None, :]) % (2 * F)
    angle = phase.astype(np.float64) * (math.pi / F)
    scale = 1.0 / math.sqrt(F)
    both = np.stack([np.cos(angle) * scale, -np.sin(angle) * scale])
    both = both.reshape(2, CHUNKS, LANES, LAG).transpose(1, 0, 2, 3)
    return both.reshape(2 * F, LAG).astype(np.float32).astype(jnp.bfloat16)


def half_products(second, row_slots, col_slots, row_places, col_places, rmask, cmask, scratch, half, block, span, emit):
    left, right, col_sum, col_diff, row_sum = scratch
    at = tuple(lax.axis_index(name) for name in AXES)
    own = 1 - at[2] if second else at[2]
    per_shard = row_slots[0].shape[1] // LANES
    first_row = span * half if second else 0

    mask = rmask[own]
    for ref, place in zip(row_slots, row_places):
        shard = place(*at)
        for i in range(per_shard):
            data = ref[first_row : first_row + span * half, i * LANES : (i + 1) * LANES]
            left[shard * per_shard + i] = data.astype(jnp.float32) * mask
    mask = cmask[own]
    for ref, place in zip(col_slots, col_places):
        shard = place(*at)
        for i in range(per_shard):
            right[shard * per_shard + i] = ref[:, i * LANES : (i + 1) * LANES].astype(jnp.float32) * mask

    def one_chunk(chunk, carry):
        for b in range(3):
            c, e = right[2 * b * CHUNKS + chunk], right[(2 * b + 1) * CHUNKS + chunk]
            col_sum[b] = c + e
            col_diff[b] = c - e
        for a in range(3):
            row_sum[a] = left[2 * a * CHUNKS + chunk] + left[(2 * a + 1) * CHUNKS + chunk]
        for a in range(3):
            one, two, three = {}, {}, {}
            for w in range(span):
                rows = slice(w * block, (w + 1) * block)
                c = [right[2 * b * CHUNKS + chunk, rows] for b in range(3)]
                plus = [col_sum[b, rows] for b in range(3)]
                minus = [col_diff[b, rows] for b in range(3)]
                for s in range(half):
                    r = w * half + s
                    p = jnp.broadcast_to(left[2 * a * CHUNKS + chunk, r : r + 1], (block, LANES))
                    q = jnp.broadcast_to(left[(2 * a + 1) * CHUNKS + chunk, r : r + 1], (block, LANES))
                    pq = jnp.broadcast_to(row_sum[a, r : r + 1], (block, LANES))
                    for b in range(3):
                        x, y, z = pq * c[b], p * plus[b], q * minus[b]
                        one[s, b] = x if w == 0 else one[s, b] + x
                        two[s, b] = y if w == 0 else two[s, b] + y
                        three[s, b] = z if w == 0 else three[s, b] + z
            for pair in range(half // 2):
                for b in range(3):
                    keys = [(2 * pair, b), (2 * pair + 1, b)]
                    first = ((pair * 3 + a) * 3 + b) * 2 * block
                    emit(chunk, first, [one[k] - three[k] for k in keys], [one[k] - two[k] for k in keys])
        return carry

    lax.fori_loop(0, CHUNKS, one_chunk, 0)


def half_scratch(half, block, span):
    pieces = 6 * CHUNKS
    return [
        pltpu.VMEM((pieces, span * half, LANES), jnp.float32),
        pltpu.VMEM((pieces, span * block, LANES), jnp.float32),
        pltpu.VMEM((3, span * block, LANES), jnp.float32),
        pltpu.VMEM((3, span * block, LANES), jnp.float32),
        pltpu.VMEM((3, span * half, LANES), jnp.float32),
    ]


def first_half(rows, cols, rmask, cmask, row_places, col_places, half, block, span):
    n_rows, n_cols = len(rows), len(cols)
    groups = half * 9 * block

    def kernel(*refs):
        row_slots, col_slots = refs[:n_rows], refs[n_rows : n_rows + n_cols]
        rmask, cmask, real_ref, imag_ref, *scratch = refs[n_rows + n_cols :]

        def emit(chunk, first, reals, imags):
            for n in range(2):
                real_ref[chunk, first + n * block : first + (n + 1) * block] = reals[n]
                imag_ref[chunk, first + n * block : first + (n + 1) * block] = imags[n]

        half_products(
            False, row_slots, col_slots, row_places, col_places, rmask, cmask, scratch, half, block, span, emit
        )

    in_vmem = pl.BlockSpec(memory_space=pltpu.VMEM)
    return pl.pallas_call(
        kernel,
        out_shape=(jax.ShapeDtypeStruct((CHUNKS, groups, LANES), jnp.float32),) * 2,
        in_specs=[in_vmem] * (n_rows + n_cols + 2),
        out_specs=(in_vmem,) * 2,
        scratch_shapes=half_scratch(half, block, span),
        cost_estimate=pl.CostEstimate(flops=FIRST_FLOPS, bytes_accessed=2**20, transcendentals=0),
        compiler_params=pltpu.CompilerParams(vmem_limit_bytes=32 * 1024 * 1024),
    )(*rows, *cols, rmask, cmask)


def correlate(rows, cols, parts, flags, table, row_places, col_places, half, block, span):
    n_rows, n_cols = len(rows), len(cols)
    groups = half * 9 * block

    def kernel(*refs):
        row_slots, col_slots = refs[:n_rows], refs[n_rows : n_rows + n_cols]
        real_ref, imag_ref, rmask, cmask, inv_ref, table_ref, out_hbm, *scratch = refs[n_rows + n_cols :]
        *scratch, cross, staged, out_sem = scratch

        def emit(chunk, first, reals, imags):
            rows = slice(first, first + 2 * block)
            re = real_ref[chunk, rows] + jnp.concatenate(reals, 0)
            im = imag_ref[chunk, rows] + jnp.concatenate(imags, 0)
            cross[chunk, rows, :LANES] = re.astype(jnp.bfloat16)
            cross[chunk, rows, LANES:] = im.astype(jnp.bfloat16)

        half_products(
            True, row_slots, col_slots, row_places, col_places, rmask, cmask, scratch, half, block, span, emit
        )
        copies = []
        for n in range(LAG // TILE):
            acc = None
            for chunk in range(CHUNKS):
                new = jnp.dot(
                    cross[chunk],
                    table_ref[2 * LANES * chunk : 2 * LANES * (chunk + 1), n * TILE : (n + 1) * TILE],
                    preferred_element_type=jnp.float32,
                )
                acc = new if acc is None else acc + new
            for s in range(half):
                inv = inv_ref[s][:, :1]
                for c in range(9):
                    group = ((s // 2) * 9 + c) * 2 + s % 2
                    staged[n, s, c] = acc[group * block : (group + 1) * block] * inv
            copies.append(pltpu.make_async_copy(staged.at[n], out_hbm.at[:, :, :, pl.ds(n * TILE, TILE)], out_sem.at[n]))
            copies[-1].start()
        for copy in copies:
            copy.wait()

    return pl.pallas_call(
        kernel,
        out_shape=jax.ShapeDtypeStruct((half, 9, block, LAG), jnp.float32),
        in_specs=[pl.BlockSpec(memory_space=pltpu.VMEM)] * (n_rows + n_cols + 6),
        out_specs=pl.BlockSpec(memory_space=pltpu.HBM),
        scratch_shapes=half_scratch(half, block, span)
        + [
            pltpu.VMEM((CHUNKS, groups, 2 * LANES), jnp.bfloat16),
            pltpu.VMEM((LAG // TILE, half, 9, block, TILE), jnp.float32),
            pltpu.SemaphoreType.DMA((LAG // TILE,)),
        ],
        compiler_params=pltpu.CompilerParams(vmem_limit_bytes=40 * 1024 * 1024),
    )(*rows, *cols, *parts, *flags, table)


def masks(usable, half, block, span):
    def kernel(usable_ref, rmask, cmask, inv_ref):
        row, col, win = (lax.axis_index(a) for a in AXES)
        usable = usable_ref[...].astype(jnp.float32)
        stations = usable.shape[1]

        def column(first, count, h):
            rows = jnp.concatenate(
                [jnp.broadcast_to(usable[w : w + 1], (count, stations)) for w in range(h * span, (h + 1) * span)], 0
            )
            shape = (span * count, stations)
            picked = lax.broadcasted_iota(jnp.int32, shape, 1) == first + lax.broadcasted_iota(jnp.int32, shape, 0) % count
            return jnp.sum(jnp.where(picked, rows, 0.0), 1, keepdims=True)

        counts = [jnp.zeros((block, LANES), jnp.float32) for _ in range(half)]
        for h in range(2):
            rm = jnp.broadcast_to(column(row * block + win * half, half, h), (span * half, LANES))
            cm = jnp.broadcast_to(column(col * block, block, h), (span * block, LANES))
            rmask[h] = rm
            cmask[h] = cm
            for w in range(span):
                for s in range(half):
                    counts[s] = counts[s] + rm[w * half + s : w * half + s + 1] * cm[w * block : (w + 1) * block]
        for s in range(half):
            inv_ref[s] = 1.0 / jnp.maximum(counts[s], 1.0)

    in_vmem = pl.BlockSpec(memory_space=pltpu.VMEM)
    shapes = ((2, span * half, LANES), (2, span * block, LANES), (half, block, LANES))
    return pl.pallas_call(
        kernel,
        out_shape=tuple(jax.ShapeDtypeStruct(shape, jnp.float32) for shape in shapes),
        in_specs=[in_vmem],
        out_specs=(in_vmem,) * 3,
        cost_estimate=pl.CostEstimate(flops=10**10, bytes_accessed=2**20, transcendentals=0),
        compiler_params=pltpu.CompilerParams(vmem_limit_bytes=4 * 1024 * 1024),
    )(usable)


def split_stations(spectra, half):
    span, block, shard = spectra.shape

    def kernel(spectra_ref, theirs_ref, mine_ref):
        data = spectra_ref[...].astype(jnp.float32)
        low = jnp.concatenate([data[w * block : w * block + half] for w in range(span)], 0)
        high = jnp.concatenate([data[w * block + half : (w + 1) * block] for w in range(span)], 0)
        first = lax.axis_index("win") == 0
        theirs_ref[...] = jnp.where(first, high, low).astype(jnp.bfloat16)
        mine_ref[: span * half] = jnp.where(first, low, high).astype(jnp.bfloat16)
        mine_ref[span * half :] = jnp.zeros((span * half, shard), jnp.bfloat16)

    in_vmem = pl.BlockSpec(memory_space=pltpu.VMEM)
    return pl.pallas_call(
        kernel,
        out_shape=(
            jax.ShapeDtypeStruct((span * half, shard), jnp.bfloat16),
            jax.ShapeDtypeStruct((2 * span * half, shard), jnp.bfloat16),
        ),
        in_specs=[in_vmem],
        out_specs=(in_vmem, in_vmem),
        compiler_params=pltpu.CompilerParams(vmem_limit_bytes=4 * 1024 * 1024),
    )(spectra.reshape(span * block, shard))


def body(spectra, usable):
    span, block, shard = spectra.shape
    n_row, n_col, n_win = (lax.axis_size(a) for a in AXES)
    assert n_row == n_col and n_win == 2
    half = block // n_win

    def send(data, move):
        pairs = []
        for r in range(n_row):
            for c in range(n_col):
                for w in range(n_win):
                    r2, c2, w2 = move(r, c, w)
                    pairs.append(((r * n_col + c) * n_win + w, (r2 * n_col + c2) * n_win + w2))
        return lax.ppermute(data, AXES, pairs)

    def other_win(r, c, w):
        return r, c, 1 - w

    flat = spectra.reshape(span * block, shard)
    turned = send(flat, lambda r, c, w: (n_row - 1 - c, r, w))
    theirs, mine = split_stations(spectra, half)
    got = send(theirs, other_win)
    flags = masks(usable, half, block, span)
    mine, *flags = lax.optimization_barrier((mine, *flags))
    mine = lax.dynamic_update_slice(mine, got, (span * half, 0))

    if n_row == 4:
        across = send(mine, lambda r, c, w: (r, c ^ 3, w))
        ready = lax.optimization_barrier((mine, turned))[0]
        beside = send(ready, lambda r, c, w: (r, c ^ 1, w))
        shifted = [across, beside, send(across, lambda r, c, w: (r, c ^ 1, w))]
        rows = [mine] + shifted
        row_places = [lambda r, c, w, k=k: c ^ k for k in (0, 3, 1, 2)]
        near = [
            turned,
            send(turned, lambda r, c, w: (r ^ 2, c, w)),
            send(turned, other_win),
            send(turned, lambda r, c, w: (r ^ 2, c, 1 - w)),
        ]
        last = lax.optimization_barrier((near[3], *shifted))[0]
        swapped = [send(x, lambda r, c, w: (r ^ 1, c, w)) for x in near[:3] + [last]]
        cols = [[*near[:2], *swapped[:2]], [*near[2:], *swapped[2:]]]
        col_places = [lambda r, c, w, e=e: n_row - 1 - (r ^ e) for e in (0, 2, 1, 3)]
    else:
        gathered = lax.all_gather(mine, "col", axis=0)
        rows = [gathered[i] for i in range(n_col)]
        row_places = [lambda r, c, w, i=i: i for i in range(n_col)]
        near = lax.all_gather(turned, "row", axis=0)
        far = send(near, other_win)
        cols = [[x[i] for i in range(n_row)] for x in (near, far)]
        col_places = [lambda r, c, w, i=i: n_row - 1 - i for i in range(n_row)]

    parts = first_half(rows, cols[0], *flags[:2], row_places, col_places, half, block, span)
    out = correlate(
        rows, cols[1], parts, flags, jnp.asarray(build_table()), row_places, col_places, half, block, span
    )
    return out.transpose(0, 2, 1, 3)


def solution(mesh):
    placed = (P("win", "row", "col"), P())
    return jax.shard_map(
        body,
        mesh=mesh,
        in_specs=placed,
        out_specs=P(("row", "win"), "col", None, None),
        check_vma=False,
    )
```

```python
import math

import jax
import jax.numpy as jnp
import numpy as np
from jax import lax
from jax.experimental import pallas as pl
from jax.experimental.pallas import tpu as pltpu
from jax.sharding import PartitionSpec as P

F = 1024
LAG = 768
DEC = 2
LANES = 128
CHUNKS = F // LANES
TILE = 256
FIRST_FLOPS = 10**9
AXES = ("row", "col", "win")


def build_table():
    shift = DEC * (np.arange(LAG, dtype=np.int64) - LAG // 2)
    phase = (np.arange(F, dtype=np.int64)[:, None] * shift[None, :]) % (2 * F)
    angle = phase.astype(np.float64) * (math.pi / F)
    scale = 1.0 / math.sqrt(F)
    both = np.stack([np.cos(angle) * scale, -np.sin(angle) * scale])
    both = both.reshape(2, CHUNKS, LANES, LAG).transpose(1, 0, 2, 3)
    return both.reshape(2 * F, LAG).astype(np.float32).astype(jnp.bfloat16)


def half_products(second, row_slots, col_slots, row_places, col_places, rmask, cmask, scratch, half, block, span, emit):
    left, right, col_sum, col_diff, row_sum = scratch
    at = tuple(lax.axis_index(name) for name in AXES)
    own = 1 - at[2] if second else at[2]
    per_shard = row_slots[0].shape[1] // LANES
    first_row = span * half if second else 0

    mask = rmask[own]
    for ref, place in zip(row_slots, row_places):
        shard = place(*at)
        for i in range(per_shard):
            data = ref[first_row : first_row + span * half, i * LANES : (i + 1) * LANES]
            left[shard * per_shard + i] = data.astype(jnp.float32) * mask
    mask = cmask[own]
    for ref, place in zip(col_slots, col_places):
        shard = place(*at)
        for i in range(per_shard):
            right[shard * per_shard + i] = ref[:, i * LANES : (i + 1) * LANES].astype(jnp.float32) * mask

    def one_chunk(chunk, carry):
        for b in range(3):
            c, e = right[2 * b * CHUNKS + chunk], right[(2 * b + 1) * CHUNKS + chunk]
            col_sum[b] = c + e
            col_diff[b] = c - e
        for a in range(3):
            row_sum[a] = left[2 * a * CHUNKS + chunk] + left[(2 * a + 1) * CHUNKS + chunk]
        for a in range(3):
            one, two, three = {}, {}, {}
            for w in range(span):
                rows = slice(w * block, (w + 1) * block)
                c = [right[2 * b * CHUNKS + chunk, rows] for b in range(3)]
                plus = [col_sum[b, rows] for b in range(3)]
                minus = [col_diff[b, rows] for b in range(3)]
                for s in range(half):
                    r = w * half + s
                    p = jnp.broadcast_to(left[2 * a * CHUNKS + chunk, r : r + 1], (block, LANES))
                    q = jnp.broadcast_to(left[(2 * a + 1) * CHUNKS + chunk, r : r + 1], (block, LANES))
                    pq = jnp.broadcast_to(row_sum[a, r : r + 1], (block, LANES))
                    for b in range(3):
                        x, y, z = pq * c[b], p * plus[b], q * minus[b]
                        one[s, b] = x if w == 0 else one[s, b] + x
                        two[s, b] = y if w == 0 else two[s, b] + y
                        three[s, b] = z if w == 0 else three[s, b] + z
            for pair in range(half // 2):
                for b in range(3):
                    keys = [(2 * pair, b), (2 * pair + 1, b)]
                    first = ((pair * 3 + a) * 3 + b) * 2 * block
                    emit(chunk, first, [one[k] - three[k] for k in keys], [one[k] - two[k] for k in keys])
        return carry

    lax.fori_loop(0, CHUNKS, one_chunk, 0, unroll=2)


def half_scratch(half, block, span):
    pieces = 6 * CHUNKS
    return [
        pltpu.VMEM((pieces, span * half, LANES), jnp.float32),
        pltpu.VMEM((pieces, span * block, LANES), jnp.float32),
        pltpu.VMEM((3, span * block, LANES), jnp.float32),
        pltpu.VMEM((3, span * block, LANES), jnp.float32),
        pltpu.VMEM((3, span * half, LANES), jnp.float32),
    ]


def first_half(rows, cols, rmask, cmask, row_places, col_places, half, block, span):
    n_rows, n_cols = len(rows), len(cols)
    groups = half * 9 * block

    def kernel(*refs):
        row_slots, col_slots = refs[:n_rows], refs[n_rows : n_rows + n_cols]
        rmask, cmask, real_ref, imag_ref, *scratch = refs[n_rows + n_cols :]

        def emit(chunk, first, reals, imags):
            for n in range(2):
                real_ref[chunk, first + n * block : first + (n + 1) * block] = reals[n]
                imag_ref[chunk, first + n * block : first + (n + 1) * block] = imags[n]

        half_products(
            False, row_slots, col_slots, row_places, col_places, rmask, cmask, scratch, half, block, span, emit
        )

    in_vmem = pl.BlockSpec(memory_space=pltpu.VMEM)
    return pl.pallas_call(
        kernel,
        out_shape=(jax.ShapeDtypeStruct((CHUNKS, groups, LANES), jnp.float32),) * 2,
        in_specs=[in_vmem] * (n_rows + n_cols + 2),
        out_specs=(in_vmem,) * 2,
        scratch_shapes=half_scratch(half, block, span),
        cost_estimate=pl.CostEstimate(flops=FIRST_FLOPS, bytes_accessed=2**20, transcendentals=0),
        compiler_params=pltpu.CompilerParams(vmem_limit_bytes=32 * 1024 * 1024),
    )(*rows, *cols, rmask, cmask)


def correlate(rows, cols, parts, flags, table, row_places, col_places, half, block, span):
    n_rows, n_cols = len(rows), len(cols)
    groups = half * 9 * block

    def kernel(*refs):
        row_slots, col_slots = refs[:n_rows], refs[n_rows : n_rows + n_cols]
        real_ref, imag_ref, rmask, cmask, inv_ref, table_ref, out_hbm, *scratch = refs[n_rows + n_cols :]
        *scratch, cross, staged, out_sem = scratch

        def emit(chunk, first, reals, imags):
            rows = slice(first, first + 2 * block)
            re = real_ref[chunk, rows] + jnp.concatenate(reals, 0)
            im = imag_ref[chunk, rows] + jnp.concatenate(imags, 0)
            cross[chunk, rows, :LANES] = re.astype(jnp.bfloat16)
            cross[chunk, rows, LANES:] = im.astype(jnp.bfloat16)

        half_products(
            True, row_slots, col_slots, row_places, col_places, rmask, cmask, scratch, half, block, span, emit
        )
        copies = []
        for n in range(LAG // TILE):
            acc = None
            for chunk in range(CHUNKS):
                new = jnp.dot(
                    cross[chunk],
                    table_ref[2 * LANES * chunk : 2 * LANES * (chunk + 1), n * TILE : (n + 1) * TILE],
                    preferred_element_type=jnp.float32,
                )
                acc = new if acc is None else acc + new
            for s in range(half):
                inv = inv_ref[s][:, :1]
                for c in range(9):
                    group = ((s // 2) * 9 + c) * 2 + s % 2
                    staged[n, s, c] = acc[group * block : (group + 1) * block] * inv
            copies.append(pltpu.make_async_copy(staged.at[n], out_hbm.at[:, :, :, pl.ds(n * TILE, TILE)], out_sem.at[n]))
            copies[-1].start()
        for copy in copies:
            copy.wait()

    return pl.pallas_call(
        kernel,
        out_shape=jax.ShapeDtypeStruct((half, 9, block, LAG), jnp.float32),
        in_specs=[pl.BlockSpec(memory_space=pltpu.VMEM)] * (n_rows + n_cols + 6),
        out_specs=pl.BlockSpec(memory_space=pltpu.HBM),
        scratch_shapes=half_scratch(half, block, span)
        + [
            pltpu.VMEM((CHUNKS, groups, 2 * LANES), jnp.bfloat16),
            pltpu.VMEM((LAG // TILE, half, 9, block, TILE), jnp.float32),
            pltpu.SemaphoreType.DMA((LAG // TILE,)),
        ],
        compiler_params=pltpu.CompilerParams(vmem_limit_bytes=40 * 1024 * 1024),
    )(*rows, *cols, *parts, *flags, table)


def masks(usable, half, block, span):
    def kernel(usable_ref, rmask, cmask, inv_ref):
        row, col, win = (lax.axis_index(a) for a in AXES)
        usable = usable_ref[...].astype(jnp.float32)
        stations = usable.shape[1]

        def column(first, count, h):
            rows = jnp.concatenate(
                [jnp.broadcast_to(usable[w : w + 1], (count, stations)) for w in range(h * span, (h + 1) * span)], 0
            )
            shape = (span * count, stations)
            picked = lax.broadcasted_iota(jnp.int32, shape, 1) == first + lax.broadcasted_iota(jnp.int32, shape, 0) % count
            return jnp.sum(jnp.where(picked, rows, 0.0), 1, keepdims=True)

        counts = [jnp.zeros((block, LANES), jnp.float32) for _ in range(half)]
        for h in range(2):
            rm = jnp.broadcast_to(column(row * block + win * half, half, h), (span * half, LANES))
            cm = jnp.broadcast_to(column(col * block, block, h), (span * block, LANES))
            rmask[h] = rm
            cmask[h] = cm
            for w in range(span):
                for s in range(half):
                    counts[s] = counts[s] + rm[w * half + s : w * half + s + 1] * cm[w * block : (w + 1) * block]
        for s in range(half):
            inv_ref[s] = 1.0 / jnp.maximum(counts[s], 1.0)

    in_vmem = pl.BlockSpec(memory_space=pltpu.VMEM)
    shapes = ((2, span * half, LANES), (2, span * block, LANES), (half, block, LANES))
    return pl.pallas_call(
        kernel,
        out_shape=tuple(jax.ShapeDtypeStruct(shape, jnp.float32) for shape in shapes),
        in_specs=[in_vmem],
        out_specs=(in_vmem,) * 3,
        cost_estimate=pl.CostEstimate(flops=10**10, bytes_accessed=2**20, transcendentals=0),
        compiler_params=pltpu.CompilerParams(vmem_limit_bytes=4 * 1024 * 1024),
    )(usable)


def split_stations(spectra, half):
    span, block, shard = spectra.shape

    def kernel(spectra_ref, theirs_ref, mine_ref):
        data = spectra_ref[...].astype(jnp.float32)
        low = jnp.concatenate([data[w * block : w * block + half] for w in range(span)], 0)
        high = jnp.concatenate([data[w * block + half : (w + 1) * block] for w in range(span)], 0)
        first = lax.axis_index("win") == 0
        theirs_ref[...] = jnp.where(first, high, low).astype(jnp.bfloat16)
        mine_ref[: span * half] = jnp.where(first, low, high).astype(jnp.bfloat16)
        mine_ref[span * half :] = jnp.zeros((span * half, shard), jnp.bfloat16)

    in_vmem = pl.BlockSpec(memory_space=pltpu.VMEM)
    return pl.pallas_call(
        kernel,
        out_shape=(
            jax.ShapeDtypeStruct((span * half, shard), jnp.bfloat16),
            jax.ShapeDtypeStruct((2 * span * half, shard), jnp.bfloat16),
        ),
        in_specs=[in_vmem],
        out_specs=(in_vmem, in_vmem),
        compiler_params=pltpu.CompilerParams(vmem_limit_bytes=4 * 1024 * 1024),
    )(spectra.reshape(span * block, shard))


def body(spectra, usable):
    span, block, shard = spectra.shape
    n_row, n_col, n_win = (lax.axis_size(a) for a in AXES)
    assert n_row == n_col and n_win == 2
    half = block // n_win

    def send(data, move):
        pairs = []
        for r in range(n_row):
            for c in range(n_col):
                for w in range(n_win):
                    r2, c2, w2 = move(r, c, w)
                    pairs.append(((r * n_col + c) * n_win + w, (r2 * n_col + c2) * n_win + w2))
        return lax.ppermute(data, AXES, pairs)

    def other_win(r, c, w):
        return r, c, 1 - w

    flat = spectra.reshape(span * block, shard)
    turned = send(flat, lambda r, c, w: ((c + 1) % n_row, r, w))
    theirs, mine = split_stations(spectra, half)
    got = send(theirs, other_win)
    flags = masks(usable, half, block, span)
    mine, *flags = lax.optimization_barrier((mine, *flags))
    mine = lax.dynamic_update_slice(mine, got, (span * half, 0))

    if n_row == 4:
        across = send(mine, lambda r, c, w: (r, c ^ 3, w))
        ready = lax.optimization_barrier((mine, turned))[0]
        beside = send(ready, lambda r, c, w: (r, c ^ 1, w))
        shifted = [across, beside, send(across, lambda r, c, w: (r, c ^ 1, w))]
        rows = [mine] + shifted
        row_places = [lambda r, c, w, k=k: c ^ k for k in (0, 3, 1, 2)]
        near = [
            turned,
            send(turned, lambda r, c, w: (r ^ 2, c, w)),
            send(turned, other_win),
            send(turned, lambda r, c, w: (r ^ 2, c, 1 - w)),
        ]
        last = lax.optimization_barrier((near[3], *shifted))[0]
        swapped = [send(x, lambda r, c, w: (r ^ 1, c, w)) for x in near[:3] + [last]]
        cols = [[*near[:2], *swapped[:2]], [*near[2:], *swapped[2:]]]
        col_places = [lambda r, c, w, e=e: lax.rem((r ^ e) + n_row - 1, n_row) for e in (0, 2, 1, 3)]
    else:
        gathered = lax.all_gather(mine, "col", axis=0)
        rows = [gathered[i] for i in range(n_col)]
        row_places = [lambda r, c, w, i=i: i for i in range(n_col)]
        near = lax.all_gather(turned, "row", axis=0)
        far = send(near, other_win)
        cols = [[x[i] for i in range(n_row)] for x in (near, far)]
        col_places = [lambda r, c, w, i=i: (i + n_row - 1) % n_row for i in range(n_row)]

    parts = first_half(rows, cols[0], *flags[:2], row_places, col_places, half, block, span)
    out = correlate(
        rows, cols[1], parts, flags, jnp.asarray(build_table()), row_places, col_places, half, block, span
    )
    return out.transpose(0, 2, 1, 3)


def solution(mesh):
    placed = (P("win", "row", "col"), P())
    return jax.shard_map(
        body,
        mesh=mesh,
        in_specs=placed,
        out_specs=P(("row", "win"), "col", None, None),
        check_vma=False,
    )
```
